32 devices in a mesh: tok: 16 (over z, y, x), ch: 2 (over core).
Axes of the slice: x: 2, y: 2, z: 4, core: 2. Of those that a mesh axis runs over, the one named last changes fastest.
Arguments:
- fields: float32 [16384, 1024], P('tok', 'ch'), may hold values from -20 to 20
- gain_one: float32 [1024], P('ch'), may hold values from 0.1 to 1.9
- tok_in_weight: float32 [3072, 16384], P('ch', 'tok'), may hold values from -0.046875 to 0.046875
- tok_in_bias: float32 [3072], P('ch'), may hold values from -3 to 3
- tok_out_weight: float32 [16384, 3072], P('tok', 'ch'), may hold values from -0.109375 to 0.109375
- gain_two: float32 [1024], P('ch'), may hold values from 0.1 to 1.9
- ch_in_weight: float32 [1024, 6144], P('tok', 'ch'), may hold values from -0.1875 to 0.1875
- ch_in_bias: float32 [6144], P('ch'), may hold values from -3 to 3
- ch_out_weight: float32 [6144, 1024], P('ch', 'tok'), may hold values from -0.078125 to 0.078125
Outputs:
- block_out: float32 [16384, 1024], P('tok', 'ch')
The draws below stay inside these ranges and needn't reach their ends.
All inputs are finite; a program needn't handle non-finite values.
Results may differ from the reference program's by a relative error of at most 0.000086.
Values sent between devices are 32-bit elements; how exact they have to be, the bound alone decides.
No kernel may reach another device: no remote copies, remote signals or barrier semaphores. Data moves between devices by JAX's collectives and lax.ppermute only.
A program may use at most 128 MiB of HBM per device.

```python
import jax
import jax.numpy as jnp
from jax import lax

TOKENS = 16384
CHANNELS = 1024
TOK_HIDDEN = 3072
CH_HIDDEN = 6144


def draw_fields(key, part):
    key_values, key_scale = jax.random.split(key, 2)
    columns = jnp.arange(CHANNELS, dtype=jnp.float32)
    base_scale = 0.3 * jnp.exp(jnp.log(3.0) * columns / (CHANNELS - 1))
    jitter = jnp.exp(jax.random.uniform(key_scale, (CHANNELS,), jnp.float32, 0.0, jnp.log(3.3)))
    scales = base_scale * jitter
    values = jnp.clip(jax.random.normal(key_values, (TOKENS, CHANNELS), jnp.float32), -6.0, 6.0)
    result = values * scales[None, :]
    return result.astype(jnp.float32)


def shard_levels(own_key, dims, cuts, smallest, largest):
    level = 1.0
    for position, parts in cuts:
        heights = jax.random.uniform(jax.random.fold_in(jax.random.fold_in(own_key, 6), position), (parts,), jnp.float32, smallest / len(cuts), largest / len(cuts))
        level = level * jnp.repeat(jnp.exp(heights), dims[position] // parts).reshape((-1,) + (1,) * (len(dims) - 1 - position))
    return level


def gaussian(rng, dims, scale, most, cuts=(), kind=jnp.bfloat16):
    array = jax.random.normal(rng, dims, jnp.float32) * scale
    if len(cuts) > 0:
        array = shard_levels(rng, dims, cuts, -0.22, 0.18) * array
    return jnp.clip(array, min=-most, max=most).astype(kind)


def setup_inputs(seed: int = 0) -> dict:
    streams_of = jax.random.split(jax.random.key(seed), 10)
    return {
        "fields": draw_fields(jax.random.fold_in(streams_of[9], 71), 0),
        "gain_one": jnp.clip(1.0 + 0.18 * jax.random.normal(streams_of[1], (CHANNELS,), jnp.float32), 0.1, 1.9),
        "tok_in_weight": gaussian(streams_of[2], (TOK_HIDDEN, TOKENS), TOKENS ** -0.5, 0.046875, ((0, 2), (1, 16)), jnp.float32),
        "tok_in_bias": gaussian(streams_of[3], (TOK_HIDDEN,), 0.5, 3.0, ((0, 2),), jnp.float32),
        "tok_out_weight": gaussian(streams_of[4], (TOKENS, TOK_HIDDEN), TOK_HIDDEN ** -0.5, 0.109375, ((0, 16), (1, 2)), jnp.float32),
        "gain_two": jnp.clip(1.0 + 0.18 * jax.random.normal(streams_of[5], (CHANNELS,), jnp.float32), 0.1, 1.9),
        "ch_in_weight": gaussian(streams_of[6], (CHANNELS, CH_HIDDEN), CHANNELS ** -0.5, 0.1875, ((0, 16), (1, 2)), jnp.float32),
        "ch_in_bias": gaussian(streams_of[7], (CH_HIDDEN,), 0.5, 3.0, ((0, 2),), jnp.float32),
        "ch_out_weight": gaussian(streams_of[8], (CH_HIDDEN, CHANNELS), CH_HIDDEN ** -0.5, 0.078125, ((0, 2), (1, 16)), jnp.float32),
    }


epsilon = 1e-05

def layer_norm(values, gain):
    centre = lax.optimization_barrier(jnp.mean(values, axis=-1, keepdims=True))
    centred = values - centre
    spread = lax.optimization_barrier(jnp.mean(centred * centred, axis=-1, keepdims=True))
    return centred * lax.rsqrt(spread + epsilon) * gain

def matmul(left, right):
    return jnp.dot(left, right, precision=lax.Precision.HIGHEST, preferred_element_type=jnp.float32)

def reference(fields, gain_one, tok_in_weight, tok_in_bias, tok_out_weight, gain_two, ch_in_weight, ch_in_bias, ch_out_weight):
    normed = layer_norm(fields, gain_one)
    hidden_tok = jax.nn.gelu(matmul(tok_in_weight, normed) + tok_in_bias[:, None], approximate=False)
    mixed_tok = fields + matmul(tok_out_weight, hidden_tok)
    normed_two = layer_norm(mixed_tok, gain_two)
    hidden_ch = jax.nn.gelu(matmul(normed_two, ch_in_weight) + ch_in_bias[None, :], approximate=False)
    return mixed_tok + matmul(hidden_ch, ch_out_weight)
```

```python
import jax
import jax.numpy as jnp
from jax import lax
from jax.sharding import PartitionSpec as P

epsilon = 1e-05
exact = lax.Precision.HIGH


def contract(left, right, left_dim, right_dim):
    return lax.dot_general(
        left,
        right,
        (((left_dim,), (right_dim,)), ((), ())),
        precision=exact,
        preferred_element_type=jnp.float32,
    )


def column_norm(values, gain):
    centre = jnp.mean(values, axis=0, keepdims=True)
    centred = values - centre
    spread = jnp.mean(centred * centred, axis=0, keepdims=True)
    return centred * lax.rsqrt(spread + epsilon) * gain


class Grid:
    def __init__(self, tok, ch):
        self.tok, self.ch = tok, ch
        self.wide = 2 if tok % 2 == 0 else 1
        self.high = 2 if tok % (2 * self.wide) == 0 else 1
        self.deep = tok // (self.wide * self.high)
        self.sizes = {"z": self.deep, "y": self.high, "x": self.wide}
        self.keys = [(c, b, a) for c in range(self.deep) for b in range(self.high) for a in range(self.wide)]

    def index(self, z, y, x):
        return (z * self.high + y) * self.wide + x

    def place(self):
        me = lax.axis_index("tok")
        return me // (self.high * self.wide), (me // self.wide) % self.high, me % self.wide

    def to_offset(self, value, offset):
        pairs = []
        for z, y, x in self.keys:
            target = (z + offset[0]) % self.deep, (y + offset[1]) % self.high, (x + offset[2]) % self.wide
            pairs.append((self.index(z, y, x), self.index(*target)))
        return lax.ppermute(value, "tok", pairs)

    def to_core(self, value, step):
        return lax.ppermute(value, "ch", [(core, (core + step) % self.ch) for core in range(self.ch)])

    def steps(self, axis):
        position = "zyx".index(axis)
        for step in range(1, self.sizes[axis]):
            yield tuple(step if slot == position else 0 for slot in range(3))

    def minus(self, offset):
        return tuple((-o) % s for o, s in zip(offset, (self.deep, self.high, self.wide)))

    def plus(self, key, offset):
        return tuple((k + o) % s for k, o, s in zip(key, offset, (self.deep, self.high, self.wide)))

    def scatter_sum(self, blocks, order):
        for axis in order:
            position = "zyx".index(axis)
            kept = [key for key in blocks if key[position] == 0]
            arrived = []
            for offset in self.steps(axis):
                sent = jnp.concatenate([blocks[self.plus(key, offset)] for key in kept], axis=0)
                arrived.append(self.to_offset(sent, offset))
            held = jnp.concatenate([blocks[key] for key in kept], axis=0)
            for value in arrived:
                held = held + value
            rows = held.shape[0] // len(kept)
            blocks = {key: held[n * rows : (n + 1) * rows] for n, key in enumerate(kept)}
        return blocks[(0, 0, 0)]

    def gather(self, block, order):
        rows = block.shape[0]
        blocks = {(0, 0, 0): block}
        for axis in order:
            keys = list(blocks)
            held = jnp.concatenate([blocks[key] for key in keys], axis=0)
            for offset in self.steps(axis):
                value = self.to_offset(held, self.minus(offset))
                for n, key in enumerate(keys):
                    blocks[self.plus(key, offset)] = value[n * rows : (n + 1) * rows]
        return jnp.concatenate([blocks[key] for key in self.keys], axis=0)


def cuts(total, parts):
    step = total // parts
    return [(n * step, total if n == parts - 1 else (n + 1) * step) for n in range(parts)]


def shards(
    grid,
    fields,
    gain_one,
    tok_in_weight,
    tok_in_bias,
    tok_out_weight,
    gain_two,
    ch_in_weight,
    ch_in_bias,
    ch_out_weight,
):
    tok, ch = grid.tok, grid.ch
    width = fields.shape[1]
    rows = ch * width // tok
    per_core = width // rows
    core = lax.axis_index("ch")
    z, y, x = grid.place()
    owners = [
        grid.index((z + c) % grid.deep, (y + b) % grid.high, (x + a) % grid.wide) for c, b, a in grid.keys
    ]

    def all_cores(value):
        return jnp.concatenate([value] + [grid.to_core(value, ch - step) for step in range(1, ch)], axis=0)

    def by_offset(value):
        starts = [(((owner // per_core - core) % ch) * per_core + owner % per_core) * rows for owner in owners]
        return jnp.concatenate([lax.dynamic_slice_in_dim(value, start, rows, 0) for start in starts], axis=0)

    def for_core(value, step):
        taken = []
        for n in range(per_core):
            owner = ((core + step) % ch) * per_core + n
            oz, oy, ox = owner // (grid.high * grid.wide), (owner // grid.wide) % grid.high, owner % grid.wide
            start = grid.index((oz - z) % grid.deep, (oy - y) % grid.high, (ox - x) % grid.wide) * rows
            taken.append(lax.dynamic_slice_in_dim(value, start, rows, 0))
        return jnp.concatenate(taken, axis=0)

    full = all_cores(fields.T)
    gains = by_offset(all_cores(gain_one[:, None])), by_offset(all_cores(gain_two[:, None]))
    full = by_offset(full)
    normed = column_norm(full, gains[0])

    hidden = tok_in_weight.shape[0]
    plans = list(zip(cuts(hidden, 3), ("xyz", "yzx", "zxy")))
    activated = []
    for (start, stop), order in plans:
        partial = contract(normed, tok_in_weight[start:stop], 1, 1)
        blocks = {key: partial[n * rows : (n + 1) * rows] for n, key in enumerate(grid.keys)}
        summed = grid.scatter_sum(blocks, order)
        activated.append(jax.nn.gelu(summed + tok_in_bias[None, start:stop], approximate=False))
    mixed_part = 0.0
    for ((start, stop), order), value in zip(plans, activated):
        mixed_part = mixed_part + contract(grid.gather(value, order[::-1]), tok_out_weight[:, start:stop], 1, 1)
    mixed = full + mixed_part
    for step in range(1, ch):
        mixed = mixed + grid.to_core(mixed_part, step)
    normed_two = column_norm(mixed, gains[1])

    first = grid.gather(ch_in_weight, "zxy")
    second = grid.gather(ch_out_weight.T, "yzx")
    hidden_sum = contract(normed_two, first, 0, 0)
    activated_two = jax.nn.gelu(hidden_sum + ch_in_bias[None, :], approximate=False)
    terms = contract(second, activated_two, 1, 1)
    result = for_core(terms + mixed, 0)
    for step in range(1, ch):
        result = result + grid.to_core(for_core(terms, step), step)
    return result.T


def solution(mesh):
    grid = Grid(mesh.shape["tok"], mesh.shape["ch"])
    in_specs = (
        P("tok", "ch"),
        P("ch"),
        P("ch", "tok"),
        P("ch"),
        P("tok", "ch"),
        P("ch"),
        P("tok", "ch"),
        P("ch"),
        P("ch", "tok"),
    )

    def block(*arrays):
        return shards(grid, *arrays)

    return jax.shard_map(block, mesh=mesh, in_specs=in_specs, out_specs=P("tok", "ch"), check_vma=False)
```

```python
import functools

import jax
import jax.numpy as jnp
from jax import lax
from jax.experimental import pallas as pl
from jax.experimental.pallas import tpu as pltpu
from jax.sharding import PartitionSpec as P

epsilon = 1e-05
exact = lax.Precision.HIGH
grant = 40 * 1024 * 1024


def contract(left, right):
    return lax.dot_general(
        left, right, (((1,), (1,)), ((), ())), precision=exact, preferred_element_type=jnp.float32
    )


def together(*values):
    return lax.optimization_barrier(values)


def halves(value):
    high = value.astype(jnp.bfloat16)
    return high, (value - high.astype(jnp.float32)).astype(jnp.bfloat16)


def three_pass(left, right):
    def product(a, b):
        return jnp.dot(a, b, preferred_element_type=jnp.float32)

    return product(left[0], right[0]) + (product(left[0], right[1]) + product(left[1], right[0]))


def column_norm(values, gain):
    centre = jnp.mean(values, axis=0, keepdims=True)
    centred = values - centre
    spread = jnp.mean(centred * centred, axis=0, keepdims=True)
    return centred * lax.rsqrt(spread + epsilon) * gain


def tile_of(size):
    return 256 if size % 256 == 0 else size


def norm_two_kernel(count, fields_ref, gain_ref, *refs):
    terms, (mixed_ref, high_ref, low_ref) = refs[:-3], refs[-3:]
    parts = []
    for piece in range(count):
        own = terms[piece :: count]
        total = own[0][...]
        for ref in own[1:]:
            total = total + ref[...]
        parts.append(total)
    mixed = fields_ref[...] + jnp.concatenate(parts, axis=0)
    mixed_ref[...] = mixed
    high_ref[...], low_ref[...] = halves(column_norm(mixed, gain_ref[...]))


def norm_two(fields, gain, terms, count):
    rows, width = fields.shape
    tile = tile_of(width)
    whole = pl.BlockSpec((rows, tile), lambda n: (0, n))
    piece = pl.BlockSpec((rows // count, tile), lambda n: (0, n))
    return pl.pallas_call(
        functools.partial(norm_two_kernel, count),
        grid=(width // tile,),
        in_specs=[whole, pl.BlockSpec((rows, 1), lambda n: (0, 0))] + [piece] * len(terms),
        out_specs=[whole] * 3,
        out_shape=[jax.ShapeDtypeStruct((rows, width), kind) for kind in (jnp.float32, jnp.bfloat16, jnp.bfloat16)],
        compiler_params=pltpu.CompilerParams(vmem_limit_bytes=grant),
        cost_estimate=pl.CostEstimate(
            flops=12 * rows * width, bytes_accessed=4 * rows * width * (4 + len(terms) // count), transcendentals=0
        ),
        name="norm_two",
    )(fields, gain, *terms)


def expand_kernel(count, high_ref, low_ref, bias_ref, *refs):
    pieces, (out_high, out_low, weight_high, weight_low) = refs[:count], refs[count:]
    depth = pieces[0].shape[0]

    @pl.when(pl.program_id(0) == 0)
    def _():
        for n, piece in enumerate(pieces):
            columns = slice(n * depth, (n + 1) * depth)
            weight_high[:, columns], weight_low[:, columns] = halves(piece[...].T)

    total = three_pass((weight_high[...], weight_low[...]), (high_ref[...], low_ref[...])) + bias_ref[...]
    active = 0.5 * total * (1.0 + lax.erf(total * 0.7071067811865476))
    out_high[...], out_low[...] = halves(active)


def expand(high, low, bias, pieces):
    depth, width = high.shape
    units = pieces[0].shape[1]
    tile = tile_of(width)
    normed = pl.BlockSpec((depth, tile), lambda n: (0, n))
    return pl.pallas_call(
        functools.partial(expand_kernel, len(pieces)),
        grid=(width // tile,),
        in_specs=[normed, normed, pl.BlockSpec((units, 1), lambda n: (0, 0))]
        + [pl.BlockSpec(piece.shape, lambda n: (0, 0)) for piece in pieces],
        out_specs=[pl.BlockSpec((units, tile), lambda n: (0, n))] * 2,
        out_shape=[jax.ShapeDtypeStruct((units, width), jnp.bfloat16)] * 2,
        scratch_shapes=[pltpu.VMEM((units, depth), jnp.bfloat16)] * 2,
        compiler_params=pltpu.CompilerParams(vmem_limit_bytes=grant),
        cost_estimate=pl.CostEstimate(
            flops=6 * units * depth * width,
            bytes_accessed=4 * (units * depth + depth * width + units * width),
            transcendentals=units * width,
        ),
        name="expand",
    )(high, low, bias, *pieces)


def reduce_kernel(places, first, high_ref, low_ref, *refs):
    count = len(places)
    pieces, refs = refs[:count], refs[count:]
    if not first:
        start_ref, refs = refs[0], refs[1:]
    out_ref, weight_high, weight_low = refs

    @pl.when(pl.program_id(0) == 0)
    def _():
        for piece, starts in zip(pieces, places):
            rows = piece.shape[0] // len(starts)
            for n, start in enumerate(starts):
                high, low = halves(piece[n * rows : (n + 1) * rows, :])
                weight_high[start : start + rows, :] = high
                weight_low[start : start + rows, :] = low

    total = three_pass((weight_high[...], weight_low[...]), (high_ref[...], low_ref[...]))
    out_ref[...] = total if first else start_ref[...] + total


def reduce(high, low, pieces, places, start):
    units, width = high.shape
    rows = sum(piece.shape[0] for piece in pieces)
    tile = tile_of(width)
    hidden = pl.BlockSpec((units, tile), lambda n: (0, n))
    total = pl.BlockSpec((rows, tile), lambda n: (0, n))
    first = start is None
    return pl.pallas_call(
        functools.partial(reduce_kernel, places, first),
        grid=(width // tile,),
        in_specs=[hidden, hidden]
        + [pl.BlockSpec(piece.shape, lambda n: (0, 0)) for piece in pieces]
        + ([] if first else [total]),
        out_specs=total,
        out_shape=jax.ShapeDtypeStruct((rows, width), jnp.float32),
        scratch_shapes=[pltpu.VMEM((rows, units), jnp.bfloat16)] * 2,
        compiler_params=pltpu.CompilerParams(vmem_limit_bytes=grant),
        cost_estimate=pl.CostEstimate(
            flops=6 * units * rows * width,
            bytes_accessed=4 * (units * rows + 2 * rows * width + units * width),
            transcendentals=0,
        ),
        name="reduce",
    )(high, low, *pieces, *([] if first else [start]))


class Grid:
    def __init__(self, tok, ch):
        self.tok, self.ch, self.deep = tok, ch, tok // 4
        self.pieces = [(b, a) for b in range(2) for a in range(2)]
        self.keys = [(c, b, a) for b, a in self.pieces for c in range(self.deep)]

    def index(self, z, y, x):
        return (z * 2 + y) * 2 + x

    def place(self, chip):
        return chip // 4, chip // 2 % 2, chip % 2

    def move(self, value, dz=0, dy=0, dx=0):
        pairs = []
        for chip in range(self.tok):
            z, y, x = self.place(chip)
            pairs.append((chip, self.index((z + dz) % self.deep, (y + dy) % 2, (x + dx) % 2)))
        return lax.ppermute(value, "tok", pairs)

    def to_core(self, value, step):
        return lax.ppermute(value, "ch", [(core, (core + step) % self.ch) for core in range(self.ch)])

    def along_z(self, value):
        return [value] + [self.move(value, dz=-step) for step in range(1, self.deep)]


def shards(
    grid,
    fields,
    gain_one,
    tok_in_weight,
    tok_in_bias,
    tok_out_weight,
    gain_two,
    ch_in_weight,
    ch_in_bias,
    ch_out_weight,
):
    ch, deep = grid.ch, grid.deep
    width = fields.shape[1]
    rows = ch * width // grid.tok
    per_core = width // rows
    core = lax.axis_index("ch")
    z, y, x = grid.place(lax.axis_index("tok"))
    owners = [grid.index((z + c) % deep, (y + b) % 2, (x + a) % 2) for c, b, a in grid.keys]
    cut = lambda value, n: value[n * (value.shape[0] // 2) : (n + 1) * (value.shape[0] // 2)]

    def all_cores(value):
        return jnp.concatenate([value] + [grid.to_core(value, ch - step) for step in range(1, ch)], axis=0)

    def by_offset(value):
        starts = [(((owner // per_core - core) % ch) * per_core + owner % per_core) * rows for owner in owners]
        return jnp.concatenate([lax.dynamic_slice_in_dim(value, start, rows, 0) for start in starts], axis=0)

    def for_core(value, step):
        taken = []
        for n in range(per_core):
            oz, oy, ox = grid.place(((core + step) % ch) * per_core + n)
            start = ((((oy - y) % 2) * 2 + (ox - x) % 2) * deep + (oz - z) % deep) * rows
            taken.append(lax.dynamic_slice_in_dim(value, start, rows, 0))
        return jnp.concatenate(taken, axis=0)

    units = ch_in_weight.shape[1]
    ends = [units * n // 3 for n in range(4)]
    spans = list(zip(ends, ends[1:]))
    out_rows = ch_out_weight.T
    in_bias = ch_in_bias[:, None]
    second_own = [out_rows[:, a:b] for a, b in spans]

    full = all_cores(fields.T)
    gains = by_offset(all_cores(gain_one[:, None])), by_offset(all_cores(gain_two[:, None]))
    first_z = grid.along_z(ch_in_weight)
    last_y = grid.move(second_own[2], dy=1)
    full = by_offset(full)
    normed = column_norm(full, gains[0])
    normed, last_y = together(normed, last_y)
    last_pair = jnp.concatenate([second_own[2], last_y], axis=0)
    last_x = grid.move(last_pair, dx=1)

    quarter = normed.shape[0] // 4
    piece = [normed[n * quarter : (n + 1) * quarter] for n in range(4)]
    middle = tok_in_weight.shape[0] // 2
    weight_a, weight_b = tok_in_weight[:middle], tok_in_weight[middle:]
    sent_a = grid.move(contract(jnp.concatenate([piece[1], piece[3]], axis=0), weight_a), dx=1)
    sent_b = grid.move(contract(cut(normed, 1), weight_b), dy=1)
    kept_a = contract(jnp.concatenate([piece[0], piece[2]], axis=0), weight_a)
    kept_b = contract(cut(normed, 0), weight_b)

    sent_a, sent_b, last_x = together(sent_a, sent_b, last_x)
    part_a, part_b = kept_a + sent_a, kept_b + sent_b
    sent_a, sent_b = grid.move(cut(part_a, 1), dy=1), grid.move(cut(part_b, 1), dx=1)
    sent_a, sent_b, *first_z = together(sent_a, sent_b, *first_z)
    partial = jnp.concatenate([cut(part_a, 0) + sent_a, cut(part_b, 0) + sent_b], axis=1)
    sent = [grid.move(partial[step * rows : (step + 1) * rows], dz=step) for step in range(1, deep)]
    line = [jnp.concatenate([value[:, a:b] for value in first_z], axis=0) for a, b in spans]
    first_x = [grid.move(line[n], dx=1) for n in range(2)]
    first_y = {2: grid.move(line[2], dy=1)}

    *sent, first_x[0] = together(*sent, first_x[0])
    summed = partial[:rows]
    for value in sent:
        summed = summed + value
    activated = jax.nn.gelu(summed + tok_in_bias[None, :], approximate=False)
    active_z = grid.along_z(activated)
    first_xy = {0: (grid.move(line[0], dy=1), grid.move(first_x[0], dy=1))}

    *active_z, second_z = together(*active_z, jnp.concatenate(second_own[:2], axis=1))
    active = jnp.concatenate(active_z, axis=0)
    active_a, active_b = active[:, :middle], active[:, middle:]
    second_z = grid.along_z(second_z)
    step_a, step_b = grid.move(active_a, dy=1), grid.move(active_b, dx=1)
    step_a, step_b = together(step_a, step_b)
    all_a = [active_a, grid.move(active_a, dx=1), step_a, grid.move(step_a, dx=1)]
    all_b = [active_b, step_b, grid.move(active_b, dy=1), grid.move(step_b, dy=1)]
    fenced = together(all_a[1], all_a[3], all_b[2], all_b[3], *second_z, *first_xy[0], first_x[1], first_y[2], last_x)
    all_a[1], all_a[3], all_b[2], all_b[3] = fenced[:4]
    second_z = fenced[4 : 4 + deep]
    first_xy[0] = fenced[4 + deep : 6 + deep]
    first_x[1], first_y[2], last_x = fenced[6 + deep :]

    first_xy[1] = grid.move(line[1], dy=1), grid.move(first_x[1], dy=1)
    first_xy[2] = grid.move(line[2], dx=1), grid.move(first_y[2], dx=1)
    last_block = jnp.concatenate([last_pair, last_x], axis=0)
    last_z = grid.along_z(last_block)
    size = spans[0][1]
    line_two = [jnp.concatenate([v[:, :size] for v in second_z], axis=0), jnp.concatenate([v[:, size:] for v in second_z], axis=0)]

    terms = [
        contract(a, tok_out_weight[:, :middle]) + contract(b, tok_out_weight[:, middle:])
        for a, b in zip(all_a, all_b)
    ]
    arrived = [grid.to_core(value, step) for step in range(1, ch) for value in terms]
    mixed, high, low = norm_two(full, gains[1], terms + arrived, 4)

    biases = [in_bias[a:b] for a, b in spans]
    hidden = {0: expand(high, low, biases[0], [line[0], first_x[0], *first_xy[0]])}
    *first_xy[1], line_two[0] = together(*first_xy[1], line_two[0])
    *first_xy[2], line_two[1] = together(*first_xy[2], line_two[1])
    second_y = grid.move(line_two[0], dy=1)
    second_x = grid.move(line_two[1], dx=1)
    hidden[1] = expand(high, low, biases[1], [line[1], first_x[1], *first_xy[1]])
    hidden[2] = expand(high, low, biases[2], [line[2], first_xy[2][0], first_y[2], first_xy[2][1]])
    second_yx = grid.move(line_two[0], dx=1), grid.move(second_y, dx=1)
    second_xy = grid.move(line_two[1], dy=1), grid.move(second_x, dy=1)

    block = rows * deep
    plain = [[n * block] for n in range(4)]
    across = [[((b * 2 + a) * deep + c) * rows for a in range(2) for b in range(2)] for c in range(deep)]
    total = reduce(*hidden[2], last_z, across, None)
    total = reduce(*hidden[0], [line_two[0], second_yx[0], second_y, second_yx[1]], plain, total)
    total = reduce(*hidden[1], [line_two[1], second_x, *second_xy], plain, total)

    result = for_core(total + mixed, 0)
    for step in range(1, ch):
        result = result + grid.to_core(for_core(total, step), step)
    return result.T


def solution(mesh):
    grid = Grid(mesh.shape["tok"], mesh.shape["ch"])
    in_specs = (
        P("tok", "ch"),
        P("ch"),
        P("ch", "tok"),
        P("ch"),
        P("tok", "ch"),
        P("ch"),
        P("tok", "ch"),
        P("ch"),
        P("ch", "tok"),
    )

    def block(*arrays):
        return shards(grid, *arrays)

    return jax.shard_map(block, mesh=mesh, in_specs=in_specs, out_specs=P("tok", "ch"), check_vma=False)
```

```python
import functools

import jax
import jax.numpy as jnp
from jax import lax
from jax.experimental import pallas as pl
from jax.experimental.pallas import tpu as pltpu
from jax.sharding import PartitionSpec as P

epsilon = 1e-05
exact = lax.Precision.HIGH
grant = 40 * 1024 * 1024


light = pl.CostEstimate(flops=0, bytes_accessed=0, transcendentals=0)


def contract(left, right):
    return lax.dot_general(
        left, right, (((1,), (1,)), ((), ())), precision=exact, preferred_element_type=jnp.float32
    )


def empty_kernel(*refs):
    pass


def fence(*values):
    anywhere = [pl.BlockSpec(memory_space=pl.ANY)] * len(values)
    return pl.pallas_call(
        empty_kernel,
        in_specs=anywhere,
        out_specs=anywhere,
        out_shape=[jax.ShapeDtypeStruct(value.shape, value.dtype) for value in values],
        input_output_aliases={n: n for n in range(len(values))},
        cost_estimate=light,
        name="fence",
    )(*values)


def halves(value):
    high = value.astype(jnp.bfloat16)
    return high, (value - high.astype(jnp.float32)).astype(jnp.bfloat16)


def three_pass(left, right):
    def product(a, b):
        return jnp.dot(a, b, preferred_element_type=jnp.float32)

    return product(left[0], right[0]) + (product(left[0], right[1]) + product(left[1], right[0]))


def column_norm(values, gain):
    centre = jnp.mean(values, axis=0, keepdims=True)
    centred = values - centre
    spread = jnp.mean(centred * centred, axis=0, keepdims=True)
    return centred * lax.rsqrt(spread + epsilon) * gain


def tile_of(size):
    return 256 if size % 256 == 0 else size


class Grid:
    def __init__(self, tok, ch):
        self.tok, self.ch, self.deep = tok, ch, tok // 4
        self.keys = [(c, b, a) for b in range(2) for a in range(2) for c in range(self.deep)]

    def index(self, z, y, x):
        return (z * 2 + y) * 2 + x

    def place(self, chip):
        return chip // 4, chip // 2 % 2, chip % 2

    def move(self, value, dz=0, dy=0, dx=0):
        pairs = []
        for chip in range(self.tok):
            z, y, x = self.place(chip)
            pairs.append((chip, self.index((z + dz) % self.deep, (y + dy) % 2, (x + dx) % 2)))
        return lax.ppermute(value, "tok", pairs)

    def to_core(self, value, step):
        return lax.ppermute(value, "ch", [(core, (core + step) % self.ch) for core in range(self.ch)])

    def line(self, own, arrived):
        return [own] + list(arrived)[::-1]

    def segments(self, orders, rows):
        where = {key: (n, m * rows) for n, order in enumerate(orders) for m, key in enumerate(order)}
        groups = []
        for start in range(0, len(self.keys), self.deep):
            group = []
            for key in self.keys[start : start + self.deep]:
                piece, row = where[key]
                if group and group[-1][0] == piece and group[-1][1] + group[-1][2] == row:
                    group[-1] = piece, group[-1][1], group[-1][2] + rows
                else:
                    group.append((piece, row, rows))
            groups.append(group)
        return groups


def block_starts(grid, place_ref, rows, per_core):
    z, y, x, core = (place_ref[n] for n in range(4))
    starts = []
    for c, b, a in grid.keys:
        owner = grid.index(lax.rem(z + c, grid.deep), lax.rem(y + b, 2), lax.rem(x + a, 2))
        half = lax.rem(lax.div(owner, per_core) + grid.ch - core, grid.ch)
        starts.append(pl.multiple_of((half * per_core + lax.rem(owner, per_core)) * rows, rows))
    return starts


def norm_one_kernel(grid, rows, per_core, place_ref, gain_ref, *refs):
    sources, (fields_ref, normed_ref, raw, ready) = refs[: grid.ch], refs[grid.ch :]
    values = jnp.concatenate([ref[...].T for ref in sources], axis=0)
    raw[...] = values
    ready[...] = column_norm(values, gain_ref[...])
    for n, start in enumerate(block_starts(grid, place_ref, rows, per_core)):
        target = slice(n * rows, (n + 1) * rows)
        fields_ref[target, :] = raw[pl.ds(start, rows), :]
        normed_ref[target, :] = ready[pl.ds(start, rows), :]


def norm_one(grid, place, gain, sources, per_core):
    height, width = sources[0].shape
    channels = width * grid.ch
    tile = tile_of(height)
    whole = pl.BlockSpec((channels, tile), lambda n, place: (0, n))
    return pl.pallas_call(
        functools.partial(norm_one_kernel, grid, channels // grid.tok, per_core),
        grid_spec=pltpu.PrefetchScalarGridSpec(
            num_scalar_prefetch=1,
            grid=(height // tile,),
            in_specs=[pl.BlockSpec((channels, 1), lambda n, place: (0, 0))]
            + [pl.BlockSpec((tile, width), lambda n, place: (n, 0))] * grid.ch,
            out_specs=[whole] * 2,
            scratch_shapes=[pltpu.VMEM((channels, tile), jnp.float32)] * 2,
        ),
        out_shape=[jax.ShapeDtypeStruct((channels, height), jnp.float32)] * 2,
        compiler_params=pltpu.CompilerParams(vmem_limit_bytes=grant),
        cost_estimate=light,
        name="norm_one",
    )(place, gain, *sources)


def project_kernel(plan, weight_ref, *refs):
    count = 1 + max(piece for _, _, groups in plan for group in groups for piece, _, _ in group)
    pieces, (out_ref, active_high, active_low) = refs[:count], refs[count:]

    @pl.when(pl.program_id(0) == 0)
    def _():
        for first, last, groups in plan:
            row = 0
            for group in groups:
                for piece, start, rows in group:
                    high, low = halves(pieces[piece][start : start + rows, :])
                    active_high[row : row + rows, first:last] = high
                    active_low[row : row + rows, first:last] = low
                    row += rows

    weight = halves(weight_ref[...].T)
    out_ref[...] = three_pass((active_high[...], active_low[...]), weight)


def project(weight, pieces, plan):
    width, units = weight.shape
    rows = sum(rows for group in plan[0][2] for _, _, rows in group)
    tile = tile_of(width)
    return pl.pallas_call(
        functools.partial(project_kernel, plan),
        grid=(width // tile,),
        in_specs=[pl.BlockSpec((tile, units), lambda n: (n, 0))]
        + [pl.BlockSpec(piece.shape, lambda n: (0, 0)) for piece in pieces],
        out_specs=pl.BlockSpec((rows, tile), lambda n: (0, n)),
        out_shape=jax.ShapeDtypeStruct((rows, width), jnp.float32),
        scratch_shapes=[pltpu.VMEM((rows, units), jnp.bfloat16)] * 2,
        compiler_params=pltpu.CompilerParams(vmem_limit_bytes=grant),
        cost_estimate=light,
        name="project",
    )(weight, *pieces)


def norm_two_kernel(grid, rows, per_core, place_ref, gain_ref, fields_ref, *refs):
    terms, (mixed_ref, high_ref, low_ref) = refs[:-3], refs[-3:]
    starts = block_starts(grid, place_ref, rows, per_core)
    gain = jnp.concatenate([gain_ref[pl.ds(start, rows), :] for start in starts], axis=0)
    total = terms[0][...]
    for ref in terms[1:]:
        total = total + ref[...]
    mixed = fields_ref[...] + total
    mixed_ref[...] = mixed
    high_ref[...], low_ref[...] = halves(column_norm(mixed, gain))


def norm_two(grid, place, gain, fields, terms, per_core):
    channels, width = fields.shape
    tile = tile_of(width)
    whole = pl.BlockSpec((channels, tile), lambda n, place: (0, n))
    return pl.pallas_call(
        functools.partial(norm_two_kernel, grid, channels // grid.tok, per_core),
        grid_spec=pltpu.PrefetchScalarGridSpec(
            num_scalar_prefetch=1,
            grid=(width // tile,),
            in_specs=[pl.BlockSpec((channels, 1), lambda n, place: (0, 0))] + [whole] * (1 + len(terms)),
            out_specs=[whole] * 3,
        ),
        out_shape=[
            jax.ShapeDtypeStruct((channels, width), kind) for kind in (jnp.float32, jnp.bfloat16, jnp.bfloat16)
        ],
        compiler_params=pltpu.CompilerParams(vmem_limit_bytes=grant),
        cost_estimate=light,
        name="norm_two",
    )(place, gain, fields, *terms)


def expand_kernel(groups, count, high_ref, low_ref, bias_ref, *refs):
    pieces, (out_high, out_low, weight_high, weight_low) = refs[:count], refs[count:]

    @pl.when(pl.program_id(0) == 0)
    def _():
        column = 0
        for group in groups:
            value = jnp.concatenate([pieces[n][start : start + rows, :] for n, start, rows in group], axis=0)
            columns = slice(column, column + value.shape[0])
            weight_high[:, columns], weight_low[:, columns] = halves(value.T)
            column += value.shape[0]

    total = three_pass((weight_high[...], weight_low[...]), (high_ref[...], low_ref[...])) + bias_ref[...]
    active = 0.5 * total * (1.0 + lax.erf(total * 0.7071067811865476))
    out_high[...], out_low[...] = halves(active)


def expand(high, low, bias, pieces, groups):
    depth, width = high.shape
    units = pieces[0].shape[1]
    tile = tile_of(width)
    normed = pl.BlockSpec((depth, tile), lambda n: (0, n))
    return pl.pallas_call(
        functools.partial(expand_kernel, groups, len(pieces)),
        grid=(width // tile,),
        in_specs=[normed, normed, pl.BlockSpec((units, 1), lambda n: (0, 0))]
        + [pl.BlockSpec(piece.shape, lambda n: (0, 0)) for piece in pieces],
        out_specs=[pl.BlockSpec((units, tile), lambda n: (0, n))] * 2,
        out_shape=[jax.ShapeDtypeStruct((units, width), jnp.bfloat16)] * 2,
        scratch_shapes=[pltpu.VMEM((units, depth), jnp.bfloat16)] * 2,
        compiler_params=pltpu.CompilerParams(vmem_limit_bytes=grant),
        cost_estimate=light,
        name="expand",
    )(high, low, bias, *pieces)


def reduce_kernel(groups, count, first, high_ref, low_ref, *refs):
    pieces, refs = refs[:count], refs[count:]
    if not first:
        start_ref, refs = refs[0], refs[1:]
    out_ref, weight_high, weight_low = refs

    @pl.when(pl.program_id(0) == 0)
    def _():
        row = 0
        for group in groups:
            for piece, start, rows in group:
                high, low = halves(pieces[piece][start : start + rows, :])
                weight_high[row : row + rows, :] = high
                weight_low[row : row + rows, :] = low
                row += rows

    total = three_pass((weight_high[...], weight_low[...]), (high_ref[...], low_ref[...]))
    out_ref[...] = total if first else start_ref[...] + total


def reduce(high, low, pieces, groups, start):
    units, width = high.shape
    rows = sum(piece.shape[0] for piece in pieces)
    tile = tile_of(width)
    hidden = pl.BlockSpec((units, tile), lambda n: (0, n))
    total = pl.BlockSpec((rows, tile), lambda n: (0, n))
    first = start is None
    return pl.pallas_call(
        functools.partial(reduce_kernel, groups, len(pieces), first),
        grid=(width // tile,),
        in_specs=[hidden, hidden]
        + [pl.BlockSpec(piece.shape, lambda n: (0, 0)) for piece in pieces]
        + ([] if first else [total]),
        out_specs=total,
        out_shape=jax.ShapeDtypeStruct((rows, width), jnp.float32),
        scratch_shapes=[pltpu.VMEM((rows, units), jnp.bfloat16)] * 2,
        compiler_params=pltpu.CompilerParams(vmem_limit_bytes=grant),
        cost_estimate=light,
        name="reduce",
    )(high, low, *pieces, *([] if first else [start]))


def join(values, axis=0):
    return jnp.concatenate(list(values), axis=axis)


def shards(
    grid,
    fields,
    gain_one,
    tok_in_weight,
    tok_in_bias,
    tok_out_weight,
    gain_two,
    ch_in_weight,
    ch_in_bias,
    ch_out_weight,
):
    ch, deep, move = grid.ch, grid.deep, grid.move
    width = fields.shape[1]
    rows = ch * width // grid.tok
    per_core = width // rows
    core = lax.axis_index("ch")
    z, y, x = grid.place(lax.axis_index("tok"))
    place = jnp.stack([z, y, x, core]).astype(jnp.int32)

    def for_core(value, step):
        taken = []
        for n in range(per_core):
            oz, oy, ox = grid.place(((core + step) % ch) * per_core + n)
            start = ((((oy - y) % 2) * 2 + (ox - x) % 2) * deep + (oz - z) % deep) * rows
            taken.append(lax.dynamic_slice_in_dim(value, start, rows, 0))
        return join(taken)

    def keys(outer, inner, low=0, high=2):
        fixed = {"y": range(2), "x": range(2), "z": range(deep), outer: range(low, high)}
        names = outer + inner
        return [
            (dict(zip(names, key))["z"], dict(zip(names, key))["y"], dict(zip(names, key))["x"])
            for key in ((o, m, i) for o in fixed[names[0]] for m in fixed[names[1]] for i in fixed[names[2]])
        ]

    y_last = grid.segments([keys("y", "xz", 0, 1), keys("y", "xz", 1, 2)], rows)
    x_last = grid.segments([keys("x", "yz", 0, 1), keys("x", "yz", 1, 2)], rows)
    z_after_xy = grid.segments([keys("z", "yx", n, n + 1) for n in range(deep)], rows)
    z_after_yx = grid.segments([keys("z", "xy", n, n + 1) for n in range(deep)], rows)

    units = ch_in_weight.shape[1]
    ends = [units * n // 3 for n in range(4)]
    spans = list(zip(ends, ends[1:]))
    out_rows = ch_out_weight.T
    in_bias = ch_in_bias[:, None]
    size = ends[1]

    others = [grid.to_core(fields, ch - step) for step in range(1, ch)]
    pair_gain = jnp.stack([gain_one, gain_two])
    gains = join([pair_gain] + [grid.to_core(pair_gain, ch - step) for step in range(1, ch)], 1).T
    own = join([ch_in_weight[:, : ends[2]], out_rows[:, : ends[2]]])
    in_last, out_last = ch_in_weight[:, ends[2] :], out_rows[:, ends[2] :]
    ring = [move(own, dz=1)]
    in_step, out_step = move(in_last, dx=1), move(out_last, dy=1)
    full, normed = norm_one(grid, place, gains[:, :1], [fields] + others, per_core)
    normed, ring[0], in_step, out_step = fence(normed, ring[0], in_step, out_step)
    ring.append(move(ring[0], dz=1))
    in_last, out_last = join([in_last, in_step]), join([out_last, out_step])
    in_step, out_step = move(in_last, dy=1), move(out_last, dx=1)

    quarter = normed.shape[0] // 4
    piece = [normed[n * quarter : (n + 1) * quarter] for n in range(4)]
    middle = tok_in_weight.shape[0] // 2
    weight_a, weight_b = tok_in_weight[:middle], tok_in_weight[middle:]
    sent_a = move(contract(join([piece[1], piece[3]]), weight_a), dx=1)
    sent_b = move(contract(normed[2 * quarter :], weight_b), dy=1)
    kept_a = contract(join([piece[0], piece[2]]), weight_a)
    kept_b = contract(normed[: 2 * quarter], weight_b)
    sent_a, sent_b, ring[1] = fence(sent_a, sent_b, ring[1])
    part_a, part_b = kept_a + sent_a, kept_b + sent_b
    sent_a, sent_b = move(part_a[quarter:], dy=1), move(part_b[quarter:], dx=1)
    for _ in range(2, deep - 1):
        ring.append(move(ring[-1], dz=1))
    sent_a, sent_b, in_step, out_step, *ring = fence(sent_a, sent_b, in_step, out_step, *ring)

    lines = grid.line(own, ring)
    first = [join([value[:rows, a:b] for value in lines]) for a, b in spans[:2]]
    second = [join([value[rows:, a:b] for value in lines]) for a, b in spans[:2]]
    in_last, out_last = join([in_last, in_step]), join([out_last, out_step])
    partial = join([part_a[:quarter] + sent_a, part_b[:quarter] + sent_b], 1)
    total = partial[(deep - 1) * rows :]
    for step in range(2, deep + 1):
        total = move(total, dz=1) + partial[(deep - step) * rows : (deep - step + 1) * rows]
    first_step = [move(first[0], dx=1), move(first[1], dy=1)]
    activated = jax.nn.gelu(total + tok_in_bias[None, :], approximate=False)

    activated, *first_step = fence(activated, *first_step)
    ring = []
    for step in range(1, deep):
        ring.append(move(ring[-1] if ring else activated, dz=1))
    second_step = [move(second[0], dy=1), move(second[1], dx=1)]
    *ring, second_step[0], second_step[1] = fence(*ring, *second_step)

    active = join(grid.line(activated, ring))
    active_a, active_b = active[:, :middle], active[:, middle:]
    step_a, step_b = move(active_a, dy=1), move(active_b, dx=1)
    in_ring = [move(in_last, dz=1)]
    step_a, step_b, in_ring[0] = fence(step_a, step_b, in_ring[0])
    active_a, active_b = join([active_a, step_a]), join([active_b, step_b])
    step_a, step_b = move(active_a, dx=1), move(active_b, dy=1)
    in_ring.append(move(in_ring[0], dz=1))
    step_a, step_b, in_ring[1] = fence(step_a, step_b, in_ring[1])

    for _ in range(2, deep - 1):
        in_ring.append(move(in_ring[-1], dz=1))
    first = [join([own, step]) for own, step in zip(first, first_step)]
    second = [join([own, step]) for own, step in zip(second, second_step)]
    first_step = [move(first[0], dy=1), move(first[1], dx=1)]
    out_ring = [move(out_last, dz=1)]
    terms = project(
        tok_out_weight,
        [active_a, step_a, active_b, step_b],
        [
            (0, middle, x_last),
            (middle, 2 * middle, [[(n + 2, start, many) for n, start, many in group] for group in y_last]),
        ],
    )
    terms = [terms] + [grid.to_core(terms, step) for step in range(1, ch)]
    mixed, high, low = norm_two(grid, place, gains[:, 1:], full, terms, per_core)

    high, first_step[0], first_step[1], out_ring[0], *in_ring = fence(high, *first_step, out_ring[0], *in_ring)
    second_step = [move(second[0], dx=1), move(second[1], dy=1)]
    out_ring.append(move(out_ring[0], dz=1))
    biases = [in_bias[a:b] for a, b in spans]
    hidden = [
        expand(high, low, biases[0], [first[0], first_step[0]], y_last),
        expand(high, low, biases[1], [first[1], first_step[1]], x_last),
    ]
    hidden_high, out_ring[1] = fence(hidden[1][0], out_ring[1])
    hidden[1] = hidden_high, hidden[1][1]
    for _ in range(2, deep - 1):
        out_ring.append(move(out_ring[-1], dz=1))
    hidden.append(expand(high, low, biases[2], grid.line(in_last, in_ring), z_after_xy))
    result = reduce(*hidden[0], [second[0], second_step[0]], x_last, None)
    result = reduce(*hidden[1], [second[1], second_step[1]], y_last, result)
    result = reduce(*hidden[2], grid.line(out_last, out_ring), z_after_yx, result)

    own_part = for_core(result + mixed, 0)
    for step in range(1, ch):
        own_part = own_part + grid.to_core(for_core(result, step), step)
    return own_part.T


def solution(mesh):
    grid = Grid(mesh.shape["tok"], mesh.shape["ch"])
    in_specs = (
        P("tok", "ch"),
        P("ch"),
        P("ch", "tok"),
        P("ch"),
        P("tok", "ch"),
        P("ch"),
        P("tok", "ch"),
        P("ch"),
        P("ch", "tok"),
    )

    def block(*arrays):
        return shards(grid, *arrays)

    return jax.shard_map(block, mesh=mesh, in_specs=in_specs, out_specs=P("tok", "ch"), check_vma=False)
```

```python
import functools

import jax
import jax.numpy as jnp
from jax import lax
from jax.experimental import pallas as pl
from jax.experimental.pallas import tpu as pltpu
from jax.sharding import PartitionSpec as P

epsilon = 1e-05
grant = 255 * 1024 * 256


light = pl.CostEstimate(flops=0, bytes_accessed=0, transcendentals=0)


def empty_kernel(*refs):
    pass


def fence(*values):
    anywhere = [pl.BlockSpec(memory_space=pl.ANY)] * len(values)
    return pl.pallas_call(
        empty_kernel,
        in_specs=anywhere,
        out_specs=anywhere,
        out_shape=[jax.ShapeDtypeStruct(value.shape, value.dtype) for value in values],
        input_output_aliases={n: n for n in range(len(values))},
        compiler_params=pltpu.CompilerParams(vmem_limit_bytes=grant),
        cost_estimate=light,
        name="fence",
    )(*values)


def halves(value):
    high = value.astype(jnp.bfloat16)
    return high, (value - high.astype(jnp.float32)).astype(jnp.bfloat16)


def three_pass(left, right):
    def product(a, b):
        return jnp.dot(a, b, preferred_element_type=jnp.float32)

    return product(left[0], right[0]) + (product(left[0], right[1]) + product(left[1], right[0]))


def column_norm(values, gain):
    centre = jnp.mean(values, axis=0, keepdims=True)
    centred = values - centre
    spread = jnp.mean(centred * centred, axis=0, keepdims=True)
    return centred * lax.rsqrt(spread + epsilon) * gain


def tile_of(size):
    return 256 if size % 256 == 0 else size


class Grid:
    def __init__(self, tok, ch):
        self.tok, self.ch, self.deep = tok, ch, tok // 4
        self.keys = [(c, b, a) for b in range(2) for a in range(2) for c in range(self.deep)]

    def index(self, z, y, x):
        return (z * 2 + y) * 2 + x

    def place(self, chip):
        return chip // 4, chip // 2 % 2, chip % 2

    def move(self, value, dz=0, dy=0, dx=0):
        pairs = []
        for chip in range(self.tok):
            z, y, x = self.place(chip)
            pairs.append((chip, self.index((z + dz) % self.deep, (y + dy) % 2, (x + dx) % 2)))
        return lax.ppermute(value, "tok", pairs)

    def to_core(self, value, step):
        return lax.ppermute(value, "ch", [(core, (core + step) % self.ch) for core in range(self.ch)])

    def line(self, own, arrived):
        return [own] + list(arrived)[::-1]

    def segments(self, orders, rows):
        where = {key: (n, m * rows) for n, order in enumerate(orders) for m, key in enumerate(order)}
        groups = []
        for start in range(0, len(self.keys), self.deep):
            group = []
            for key in self.keys[start : start + self.deep]:
                piece, row = where[key]
                if group and group[-1][0] == piece and group[-1][1] + group[-1][2] == row:
                    group[-1] = piece, group[-1][1], group[-1][2] + rows
                else:
                    group.append((piece, row, rows))
            groups.append(group)
        return groups


def block_starts(grid, place_ref, rows, per_core):
    z, y, x, core = (place_ref[n] for n in range(4))
    starts = []
    for c, b, a in grid.keys:
        owner = grid.index(lax.rem(z + c, grid.deep), lax.rem(y + b, 2), lax.rem(x + a, 2))
        half = lax.rem(lax.div(owner, per_core) + grid.ch - core, grid.ch)
        starts.append(pl.multiple_of((half * per_core + lax.rem(owner, per_core)) * rows, rows))
    return starts


def norm_one_kernel(grid, rows, per_core, place_ref, gain_ref, *refs):
    sources, (fields_ref, high_ref, low_ref, raw, ready) = refs[: grid.ch], refs[grid.ch :]
    values = jnp.concatenate([ref[...].T for ref in sources], axis=0)
    raw[...] = values
    ready[...] = column_norm(values, gain_ref[...])
    for n, start in enumerate(block_starts(grid, place_ref, rows, per_core)):
        target = slice(n * rows, (n + 1) * rows)
        fields_ref[target, :] = raw[pl.ds(start, rows), :]
        high_ref[target, :], low_ref[target, :] = halves(ready[pl.ds(start, rows), :])


def norm_one(grid, place, gain, sources, per_core):
    height, width = sources[0].shape
    channels = width * grid.ch
    tile = tile_of(height)
    whole = pl.BlockSpec((channels, tile), lambda n, place: (0, n))
    return pl.pallas_call(
        functools.partial(norm_one_kernel, grid, channels // grid.tok, per_core),
        grid_spec=pltpu.PrefetchScalarGridSpec(
            num_scalar_prefetch=1,
            grid=(height // tile,),
            in_specs=[pl.BlockSpec((channels, 1), lambda n, place: (0, 0))]
            + [pl.BlockSpec((tile, width), lambda n, place: (n, 0))] * grid.ch,
            out_specs=[whole] * 3,
            scratch_shapes=[pltpu.VMEM((channels, tile), jnp.float32)] * 2,
        ),
        out_shape=[
            jax.ShapeDtypeStruct((channels, height), kind) for kind in (jnp.float32, jnp.bfloat16, jnp.bfloat16)
        ],
        compiler_params=pltpu.CompilerParams(vmem_limit_bytes=grant),
        cost_estimate=light,
        name="norm_one",
    )(place, gain, *sources)


def mix_kernel(high_one, high_two, low_one, low_two, weight_ref, out_ref):
    normed = join([high_one[...], high_two[...]]), join([low_one[...], low_two[...]])
    out_ref[...] = three_pass(normed, halves(weight_ref[...].T))


def mix(high, low, weight, part, quarters):
    channels, height = high.shape
    units = weight.shape[0] // 2
    tile = tile_of(units)
    picked = [pl.BlockSpec((channels // 4, height), lambda n, q=q: (q, 0)) for q in quarters]
    return pl.pallas_call(
        mix_kernel,
        grid=(units // tile,),
        in_specs=picked * 2 + [pl.BlockSpec((tile, height), lambda n: (n + part * (units // tile), 0))],
        out_specs=pl.BlockSpec((channels // 2, tile), lambda n: (0, n)),
        out_shape=jax.ShapeDtypeStruct((channels // 2, units), jnp.float32),
        compiler_params=pltpu.CompilerParams(vmem_limit_bytes=grant),
        cost_estimate=light,
        name="mix",
    )(high, high, low, low, weight)


def stack_kernel(count, parts, *refs):
    for out_ref, (top, bottom, left, right) in zip(refs[count:], parts):
        for n, ref in enumerate(refs[:count]):
            out_ref[n * (bottom - top) : (n + 1) * (bottom - top), :] = ref[top:bottom, left:right]


def stack(values, parts):
    shapes = [(len(values) * (bottom - top), right - left) for top, bottom, left, right in parts]
    return pl.pallas_call(
        functools.partial(stack_kernel, len(values), parts),
        grid=(1,),
        in_specs=[pl.BlockSpec(value.shape, lambda n: (0, 0)) for value in values],
        out_specs=[pl.BlockSpec(shape, lambda n: (0, 0)) for shape in shapes],
        out_shape=[jax.ShapeDtypeStruct(shape, jnp.float32) for shape in shapes],
        compiler_params=pltpu.CompilerParams(vmem_limit_bytes=grant),
        cost_estimate=light,
        name="stack",
    )(*values)


def halve_kernel(kept_a, sent_a, kept_b, sent_b, *outs):
    for kept, sent, (top, bottom) in ((kept_a, sent_a, outs[:2]), (kept_b, sent_b, outs[2:])):
        total = kept[...] + sent[...]
        top[...], bottom[...] = total[: total.shape[0] // 2], total[total.shape[0] // 2 :]


def merge_kernel(kept_a, sent_a, kept_b, sent_b, *outs):
    middle = kept_a.shape[1]
    for n, out_ref in enumerate(outs):
        block = slice(n * out_ref.shape[0], (n + 1) * out_ref.shape[0])
        out_ref[:, :middle] = kept_a[block, :] + sent_a[block, :]
        out_ref[:, middle:] = kept_b[block, :] + sent_b[block, :]


def sums(kernel, values, count, shape):
    return pl.pallas_call(
        kernel,
        grid=(1,),
        in_specs=[pl.BlockSpec(value.shape, lambda n: (0, 0)) for value in values],
        out_specs=[pl.BlockSpec(shape, lambda n: (0, 0))] * count,
        out_shape=[jax.ShapeDtypeStruct(shape, jnp.float32)] * count,
        compiler_params=pltpu.CompilerParams(vmem_limit_bytes=grant),
        cost_estimate=light,
        name="sums",
    )(*values)


def project_kernel(rows, places, weight_ref, *refs):
    pieces, earlier, (out_ref, active_high, active_low) = refs[:4], refs[4:-3], refs[-3:]
    middle = pieces[0].shape[1]

    @pl.when(pl.program_id(0) == 0)
    def _():
        for n, piece in enumerate(pieces):
            active_high[n * rows : (n + 1) * rows, :], active_low[n * rows : (n + 1) * rows, :] = halves(piece[...])

    high, low = halves(weight_ref[...].T)
    sums = []
    for part in range(2):
        taken, units = slice(part * 2 * rows, (part + 1) * 2 * rows), slice(part * middle, (part + 1) * middle)
        product = three_pass((active_high[taken, :], active_low[taken, :]), (high[units, :], low[units, :]))
        sums += [product[:rows], product[rows:]]
    for group in range(out_ref.shape[0] // rows):
        target = slice(group * rows, (group + 1) * rows)
        terms = [value for value, place in zip(sums, places) if place == group]
        terms += [ref[target, :] for ref in earlier if group < ref.shape[0] // rows]
        out_ref[target, :] = functools.reduce(lambda a, b: a + b, terms)


def project(weight, pieces, places, groups, earlier=()):
    width, units = weight.shape
    rows = pieces[0].shape[0]
    tile = tile_of(width)
    return pl.pallas_call(
        functools.partial(project_kernel, rows, places),
        grid=(width // tile,),
        in_specs=[pl.BlockSpec((tile, units), lambda n: (n, 0))]
        + [pl.BlockSpec(piece.shape, lambda n: (0, 0)) for piece in pieces]
        + [pl.BlockSpec((value.shape[0], tile), lambda n: (0, n)) for value in earlier],
        out_specs=pl.BlockSpec((groups * rows, tile), lambda n: (0, n)),
        out_shape=jax.ShapeDtypeStruct((groups * rows, width), jnp.float32),
        scratch_shapes=[pltpu.VMEM((4 * rows, units // 2), jnp.bfloat16)] * 2,
        compiler_params=pltpu.CompilerParams(vmem_limit_bytes=grant),
        cost_estimate=light,
        name="project",
    )(weight, *pieces, *earlier)


def norm_two_kernel(grid, rows, per_core, place_ref, gain_ref, fields_ref, *refs):
    terms, (mixed_ref, high_ref, low_ref) = refs[:-3], refs[-3:]
    starts = block_starts(grid, place_ref, rows, per_core)
    gain = jnp.concatenate([gain_ref[pl.ds(start, rows), :] for start in starts], axis=0)
    total = terms[0][...]
    for ref in terms[1:]:
        total = total + ref[...]
    mixed = fields_ref[...] + total
    mixed_ref[...] = mixed
    high_ref[...], low_ref[...] = halves(column_norm(mixed, gain))


def norm_two(grid, place, gain, fields, terms, per_core):
    channels, width = fields.shape
    tile = tile_of(width)
    whole = pl.BlockSpec((channels, tile), lambda n, place: (0, n))
    return pl.pallas_call(
        functools.partial(norm_two_kernel, grid, channels // grid.tok, per_core),
        grid_spec=pltpu.PrefetchScalarGridSpec(
            num_scalar_prefetch=1,
            grid=(width // tile,),
            in_specs=[pl.BlockSpec((channels, 1), lambda n, place: (0, 0))] + [whole] * (1 + len(terms)),
            out_specs=[whole] * 3,
        ),
        out_shape=[
            jax.ShapeDtypeStruct((channels, width), kind) for kind in (jnp.float32, jnp.bfloat16, jnp.bfloat16)
        ],
        compiler_params=pltpu.CompilerParams(vmem_limit_bytes=grant),
        cost_estimate=light,
        name="norm_two",
    )(place, gain, fields, *terms)


def expand_kernel(groups, count, high_ref, low_ref, bias_ref, *refs):
    pieces, (out_high, out_low, weight_high, weight_low) = refs[:count], refs[count:]

    @pl.when(pl.program_id(0) == 0)
    def _():
        column = 0
        for group in groups:
            value = jnp.concatenate([pieces[n][start : start + rows, :] for n, start, rows in group], axis=0)
            columns = slice(column, column + value.shape[0])
            weight_high[:, columns], weight_low[:, columns] = halves(value.T)
            column += value.shape[0]

    total = three_pass((weight_high[...], weight_low[...]), (high_ref[...], low_ref[...])) + bias_ref[...]
    active = 0.5 * total * (1.0 + lax.erf(total * 0.7071067811865476))
    out_high[...], out_low[...] = halves(active)


def expand(high, low, bias, pieces, groups):
    depth, width = high.shape
    units = pieces[0].shape[1]
    tile = tile_of(width)
    normed = pl.BlockSpec((depth, tile), lambda n: (0, n))
    return pl.pallas_call(
        functools.partial(expand_kernel, groups, len(pieces)),
        grid=(width // tile,),
        in_specs=[normed, normed, pl.BlockSpec((units, 1), lambda n: (0, 0))]
        + [pl.BlockSpec(piece.shape, lambda n: (0, 0)) for piece in pieces],
        out_specs=[pl.BlockSpec((units, tile), lambda n: (0, n))] * 2,
        out_shape=[jax.ShapeDtypeStruct((units, width), jnp.bfloat16)] * 2,
        scratch_shapes=[pltpu.VMEM((units, depth), jnp.bfloat16)] * 2,
        compiler_params=pltpu.CompilerParams(vmem_limit_bytes=grant),
        cost_estimate=light,
        name="expand",
    )(high, low, bias, *pieces)


def reduce_kernel(groups, count, first, spread, *refs):
    if spread:
        place_ref, refs = refs[0], refs[1:]
    (high_ref, low_ref), pieces, refs = refs[:2], refs[2 : 2 + count], refs[2 + count :]
    if not first:
        start_ref, refs = refs[0], refs[1:]
    if spread:
        mixed_ref, refs = refs[0], refs[1:]
    outs, (weight_high, weight_low) = refs[:-2], refs[-2:]

    @pl.when(pl.program_id(0) == 0)
    def _():
        row = 0
        for group in groups:
            for piece, start, rows in group:
                high, low = halves(pieces[piece][start : start + rows, :])
                weight_high[row : row + rows, :] = high
                weight_low[row : row + rows, :] = low
                row += rows

    total = three_pass((weight_high[...], weight_low[...]), (high_ref[...], low_ref[...]))
    if not first:
        total = start_ref[...] + total
    if not spread:
        outs[0][...] = total
        return
    grid, rows, per_core = spread
    for n, start in enumerate(block_starts(grid, place_ref, rows, per_core)):
        block = slice(n * rows, (n + 1) * rows)
        row = pl.multiple_of(lax.rem(start, per_core * rows), rows)
        step = lax.div(start, per_core * rows)
        for core, out_ref in enumerate(outs):
            value = total[block] + mixed_ref[block, :] if core == 0 else total[block]

            @pl.when(step == core)
            def _():
                out_ref[pl.ds(row, rows), :] = value


def reduce(high, low, pieces, groups, start, spread=None, place=None, mixed=None):
    units, width = high.shape
    rows = sum(piece.shape[0] for piece in pieces)
    tile = tile_of(width)
    hidden = pl.BlockSpec((units, tile), lambda n, *_: (0, n))
    total = pl.BlockSpec((rows, tile), lambda n, *_: (0, n))
    first = start is None
    outs = spread[0].ch if spread else 1
    return pl.pallas_call(
        functools.partial(reduce_kernel, groups, len(pieces), first, spread),
        grid_spec=pltpu.PrefetchScalarGridSpec(
            num_scalar_prefetch=1 if spread else 0,
            grid=(width // tile,),
            in_specs=[hidden, hidden]
            + [pl.BlockSpec(piece.shape, lambda n, *_: (0, 0)) for piece in pieces]
            + [total] * ((not first) + (mixed is not None)),
            out_specs=[pl.BlockSpec((rows // outs, tile), lambda n, *_: (0, n))] * outs,
            scratch_shapes=[pltpu.VMEM((rows, units), jnp.bfloat16)] * 2,
        ),
        out_shape=[jax.ShapeDtypeStruct((rows // outs, width), jnp.float32)] * outs,
        compiler_params=pltpu.CompilerParams(vmem_limit_bytes=grant),
        cost_estimate=light,
        name="reduce",
    )(*([place] if spread else []), high, low, *pieces, *([] if first else [start]), *([mixed] if spread else []))


def finish_kernel(*refs):
    total = refs[0][...]
    for ref in refs[1:-1]:
        total = total + ref[...]
    refs[-1][...] = total.T


def finish(values):
    channels, width = values[0].shape
    tile = tile_of(width)
    return pl.pallas_call(
        finish_kernel,
        grid=(width // tile,),
        in_specs=[pl.BlockSpec((channels, tile), lambda n: (0, n))] * len(values),
        out_specs=pl.BlockSpec((tile, channels), lambda n: (n, 0)),
        out_shape=jax.ShapeDtypeStruct((width, channels), jnp.float32),
        compiler_params=pltpu.CompilerParams(vmem_limit_bytes=grant),
        cost_estimate=light,
        name="finish",
    )(*values)


def join(values, axis=0):
    return jnp.concatenate(list(values), axis=axis)


def shards(
    grid,
    fields,
    gain_one,
    tok_in_weight,
    tok_in_bias,
    tok_out_weight,
    gain_two,
    ch_in_weight,
    ch_in_bias,
    ch_out_weight,
):
    ch, deep, move = grid.ch, grid.deep, grid.move
    width = fields.shape[1]
    rows = ch * width // grid.tok
    per_core = width // rows
    core = lax.axis_index("ch")
    z, y, x = grid.place(lax.axis_index("tok"))
    place = jnp.stack([z, y, x, core]).astype(jnp.int32)

    def keys(outer, inner, low=0, high=2):
        fixed = {"y": range(2), "x": range(2), "z": range(deep), outer: range(low, high)}
        names = outer + inner
        return [
            (dict(zip(names, key))["z"], dict(zip(names, key))["y"], dict(zip(names, key))["x"])
            for key in ((o, m, i) for o in fixed[names[0]] for m in fixed[names[1]] for i in fixed[names[2]])
        ]

    def lone(outer, inner):
        return [keys(outer, inner, n, n + 1) for n in range(deep if outer == "z" else 2)]

    whole = keys("z", "yx", 0, deep)
    corner = {(b, a): [key for key in whole if key[1:] == (b, a)] for b in range(2) for a in range(2)}
    y_last = grid.segments([corner[0, 0], corner[0, 1], corner[1, 0], corner[1, 1]], rows)
    x_last = grid.segments([corner[0, 0], corner[1, 0], corner[0, 1], corner[1, 1]], rows)
    y_last_pair = grid.segments([corner[0, 0] + corner[0, 1], corner[1, 0] + corner[1, 1]], rows)
    x_last_pair = grid.segments([corner[0, 0] + corner[1, 0], corner[0, 1] + corner[1, 1]], rows)
    z_after_xy = grid.segments(lone("z", "yx"), rows)
    z_after_yx = grid.segments(lone("z", "xy"), rows)

    units = ch_in_weight.shape[1]
    ends = [units * n // 3 for n in range(4)]
    spans = list(zip(ends, ends[1:]))
    out_rows = ch_out_weight.T

    others = [grid.to_core(fields, ch - step) for step in range(1, ch)]
    pair_gain = jnp.stack([gain_one, gain_two])
    gains = join([pair_gain] + [grid.to_core(pair_gain, ch - step) for step in range(1, ch)], 1).T
    own = join([ch_in_weight[:, : ends[2]], out_rows[:, : ends[2]]])
    in_last, out_last = ch_in_weight[:, ends[2] :], out_rows[:, ends[2] :]
    ring = [move(own, dz=1)]
    in_step, out_step = move(in_last, dx=1), move(out_last, dy=1)
    full, high, low = norm_one(grid, place, gains[:, :1], [fields] + others, per_core)
    high, in_step, out_step = fence(high, in_step, out_step)
    in_last, out_last = join([in_last, in_step]), join([out_last, out_step])
    in_step, out_step = move(in_last, dy=1), move(out_last, dx=1)

    middle = tok_in_weight.shape[0] // 2
    quarter = deep * rows
    sent_a = mix(high, low, tok_in_weight, 0, (1, 3))
    sent_b = mix(high, low, tok_in_weight, 1, (2, 3))
    sent_a, sent_b, ring[0] = fence(sent_a, sent_b, ring[0])
    sent_a, sent_b = move(sent_a, dx=1), move(sent_b, dy=1)
    ring.append(move(ring[0], dz=1))
    kept_a = mix(high, low, tok_in_weight, 0, (0, 2))
    kept_b = mix(high, low, tok_in_weight, 1, (0, 1))
    biases = [ch_in_bias[a:b, None] for a, b in spans]
    sent_a, sent_b, kept_a, kept_b, in_step, out_step, ring[1], *biases = fence(
        sent_a, sent_b, kept_a, kept_b, in_step, out_step, ring[1], *biases
    )
    kept_a, sent_a, kept_b, sent_b = sums(halve_kernel, [kept_a, sent_a, kept_b, sent_b], 4, (quarter, middle))
    sent_a, sent_b = move(sent_a, dy=1), move(sent_b, dx=1)
    in_last, out_last = join([in_last, in_step]), join([out_last, out_step])
    for _ in range(2, deep - 1):
        ring.append(move(ring[-1], dz=1))
    sent_a, sent_b, in_last, out_last, ring[-1] = fence(sent_a, sent_b, in_last, out_last, ring[-1])

    partial = sums(merge_kernel, [kept_a, sent_a, kept_b, sent_b], deep, (rows, 2 * middle))
    total = partial[deep - 1]
    for step in range(2, deep + 1):
        total = move(total, dz=1) + partial[deep - step]
    lines = stack(grid.line(own, ring), [(r, r + rows, a, b) for r in (0, rows) for a, b in spans[:2]])
    first, second = [[line] for line in lines[:2]], [[line] for line in lines[2:]]
    first_step = [move(first[0][0], dx=1), move(first[1][0], dy=1)]
    activated = jax.nn.gelu(total + tok_in_bias[None, :], approximate=False)

    activated, *lines = fence(activated, first[0][0], first[1][0], *first_step)
    first = [[lines[0], lines[2]], [lines[1], lines[3]]]
    ring = []
    for step in range(1, deep):
        ring.append(move(ring[-1] if ring else activated, dz=1))
    first_step = [move(value, dy=1) for value in first[0]] + [move(value, dx=1) for value in first[1]]
    ring[-1], in_last, *first_step = fence(ring[-1], in_last, *first_step)
    first = [first[0] + first_step[:2], first[1] + first_step[2:]]

    active_a, active_b = stack(grid.line(activated, ring), [(0, rows, 0, middle), (0, rows, middle, 2 * middle)])
    step_a, step_b = move(active_a, dy=1), move(active_b, dx=1)
    in_ring = [move(in_last, dz=1)]
    step_a, step_b, in_ring[0] = fence(step_a, step_b, in_ring[0])
    arrived = [move(active_a, dx=1), move(step_a, dx=1), move(active_b, dy=1), move(step_b, dy=1)]
    in_ring.append(move(in_ring[0], dz=1))
    terms = project(tok_out_weight, [active_a, step_a, active_b, step_b], (0, 2, 0, 1), 3)
    terms, in_ring[1], *arrived = fence(terms, in_ring[1], *arrived)

    for _ in range(2, deep - 1):
        in_ring.append(move(in_ring[-1], dz=1))
    second_step = [move(second[0][0], dy=1), move(second[1][0], dx=1)]
    terms = project(tok_out_weight, arrived, (1, 3, 2, 3), 4, [terms])
    terms = [terms] + [grid.to_core(terms, step) for step in range(1, ch)]
    mixed, high, low = norm_two(grid, place, gains[:, 1:], full, terms, per_core)

    high, out_last, in_ring[-1], *second_step = fence(high, out_last, in_ring[-1], *second_step)
    second = [stack([line[0], step], [(0, quarter, 0, step.shape[1])])[0] for line, step in zip(second, second_step)]
    second_step = [move(second[0], dx=1), move(second[1], dy=1)]
    out_ring = [move(out_last, dz=1)]
    hidden = [
        expand(high, low, biases[0], first[0], y_last),
        expand(high, low, biases[1], first[1], x_last),
    ]
    hidden_high, out_ring[0] = fence(hidden[1][0], out_ring[0])
    hidden[1] = hidden_high, hidden[1][1]
    out_ring.append(move(out_ring[0], dz=1))
    hidden.append(expand(high, low, biases[2], grid.line(in_last, in_ring), z_after_xy))
    hidden_high, out_ring[1] = fence(hidden[2][0], out_ring[1])
    hidden[2] = hidden_high, hidden[2][1]
    for _ in range(2, deep - 1):
        out_ring.append(move(out_ring[-1], dz=1))
    (result,) = reduce(*hidden[0], [second[0], second_step[0]], x_last_pair, None)
    (result,) = reduce(*hidden[1], [second[1], second_step[1]], y_last_pair, result)
    spread = grid, rows, per_core
    parts = reduce(*hidden[2], grid.line(out_last, out_ring), z_after_yx, result, spread, place, mixed)
    return finish([parts[0]] + [grid.to_core(part, step) for step, part in enumerate(parts) if step])


def solution(mesh):
    grid = Grid(mesh.shape["tok"], mesh.shape["ch"])
    in_specs = (
        P("tok", "ch"),
        P("ch"),
        P("ch", "tok"),
        P("ch"),
        P("tok", "ch"),
        P("ch"),
        P("tok", "ch"),
        P("ch"),
        P("ch", "tok"),
    )

    def block(*arrays):
        return shards(grid, *arrays)

    return jax.shard_map(block, mesh=mesh, in_specs=in_specs, out_specs=P("tok", "ch"), check_vma=False)
```

```python
import functools

import jax
import jax.numpy as jnp
from jax import lax
from jax.experimental import pallas as pl
from jax.experimental.pallas import tpu as pltpu
from jax.sharding import PartitionSpec as P

epsilon = 1e-05
grant = 255 * 1024 * 256


light = pl.CostEstimate(flops=0, bytes_accessed=0, transcendentals=0)


def empty_kernel(*refs):
    pass


def fence(*values):
    anywhere = [pl.BlockSpec(memory_space=pl.ANY)] * len(values)
    return pl.pallas_call(
        empty_kernel,
        in_specs=anywhere,
        out_specs=anywhere,
        out_shape=[jax.ShapeDtypeStruct(value.shape, value.dtype) for value in values],
        input_output_aliases={n: n for n in range(len(values))},
        compiler_params=pltpu.CompilerParams(vmem_limit_bytes=grant),
        cost_estimate=light,
        name="fence",
    )(*values)


def halves(value):
    high = value.astype(jnp.bfloat16)
    return high, (value - high.astype(jnp.float32)).astype(jnp.bfloat16)


def three_pass(left, right):
    def product(a, b):
        return jnp.dot(a, b, preferred_element_type=jnp.float32)

    return product(left[0], right[0]) + (product(left[0], right[1]) + product(left[1], right[0]))


def column_norm(values, gain):
    centre = jnp.mean(values, axis=0, keepdims=True)
    centred = values - centre
    spread = jnp.mean(centred * centred, axis=0, keepdims=True)
    return centred * lax.rsqrt(spread + epsilon) * gain


def tile_of(size):
    return 256 if size % 256 == 0 else size


class Grid:
    def __init__(self, tok, ch):
        self.tok, self.ch, self.deep = tok, ch, tok // 4
        self.keys = [(c, b, a) for b in range(2) for a in range(2) for c in range(self.deep)]

    def index(self, z, y, x):
        return (z * 2 + y) * 2 + x

    def place(self, chip):
        return chip // 4, chip // 2 % 2, chip % 2

    def move(self, value, dz=0, dy=0, dx=0):
        pairs = []
        for chip in range(self.tok):
            z, y, x = self.place(chip)
            pairs.append((chip, self.index((z + dz) % self.deep, (y + dy) % 2, (x + dx) % 2)))
        return lax.ppermute(value, "tok", pairs)

    def to_core(self, value, step):
        return lax.ppermute(value, "ch", [(core, (core + step) % self.ch) for core in range(self.ch)])

    def line(self, own, arrived):
        return [own] + list(arrived)[::-1]

    def segments(self, orders, rows):
        where = {key: (n, m * rows) for n, order in enumerate(orders) for m, key in enumerate(order)}
        groups = []
        for start in range(0, len(self.keys), self.deep):
            group = []
            for key in self.keys[start : start + self.deep]:
                piece, row = where[key]
                if group and group[-1][0] == piece and group[-1][1] + group[-1][2] == row:
                    group[-1] = piece, group[-1][1], group[-1][2] + rows
                else:
                    group.append((piece, row, rows))
            groups.append(group)
        return groups


def block_starts(grid, place_ref, rows, per_core):
    z, y, x, core = (place_ref[n] for n in range(4))
    starts = []
    for c, b, a in grid.keys:
        owner = grid.index(lax.rem(z + c, grid.deep), lax.rem(y + b, 2), lax.rem(x + a, 2))
        half = lax.rem(lax.div(owner, per_core) + grid.ch - core, grid.ch)
        starts.append(pl.multiple_of((half * per_core + lax.rem(owner, per_core)) * rows, rows))
    return starts


def norm_one_kernel(grid, rows, per_core, place_ref, gain_ref, *refs):
    sources, (fields_ref, high_ref, low_ref, raw, ready) = refs[: grid.ch], refs[grid.ch :]
    values = jnp.concatenate([ref[...].T for ref in sources], axis=0)
    raw[...] = values
    ready[...] = column_norm(values, gain_ref[...])
    for n, start in enumerate(block_starts(grid, place_ref, rows, per_core)):
        target = slice(n * rows, (n + 1) * rows)
        fields_ref[target, :] = raw[pl.ds(start, rows), :]
        high_ref[target, :], low_ref[target, :] = halves(ready[pl.ds(start, rows), :])


def norm_one(grid, place, gain, sources, per_core):
    height, width = sources[0].shape
    channels = width * grid.ch
    tile = tile_of(height)
    whole = pl.BlockSpec((channels, tile), lambda n, place: (0, n))
    return pl.pallas_call(
        functools.partial(norm_one_kernel, grid, channels // grid.tok, per_core),
        grid_spec=pltpu.PrefetchScalarGridSpec(
            num_scalar_prefetch=1,
            grid=(height // tile,),
            in_specs=[pl.BlockSpec((channels, 1), lambda n, place: (0, 0))]
            + [pl.BlockSpec((tile, width), lambda n, place: (n, 0))] * grid.ch,
            out_specs=[whole] * 3,
            scratch_shapes=[pltpu.VMEM((channels, tile), jnp.float32)] * 2,
        ),
        out_shape=[
            jax.ShapeDtypeStruct((channels, height), kind) for kind in (jnp.float32, jnp.bfloat16, jnp.bfloat16)
        ],
        compiler_params=pltpu.CompilerParams(vmem_limit_bytes=grant),
        cost_estimate=light,
        name="norm_one",
    )(place, gain, *sources)


def mix_kernel(steps, high_one, high_two, low_one, low_two, weight_ref, out_a, out_b):
    normed = join([high_one[...], high_two[...]]), join([low_one[...], low_two[...]])
    product = three_pass(normed, halves(weight_ref[...].T))
    part = pl.program_id(0) // steps

    @pl.when(part == 0)
    def _():
        out_a[...] = product

    @pl.when(part == 1)
    def _():
        out_b[...] = product


def mix(high, low, weight, kept):
    channels, height = high.shape
    units = weight.shape[0] // 2
    tile = tile_of(units)
    steps = units // tile
    if kept:
        quarters = lambda n: 0, lambda n: 2 - n // steps
    else:
        quarters = lambda n: 1 + n // steps, lambda n: 3
    picked = [pl.BlockSpec((channels // 4, height), lambda n, q=q: (q(n), 0)) for q in quarters]
    return pl.pallas_call(
        functools.partial(mix_kernel, steps),
        grid=(2 * steps,),
        in_specs=picked * 2 + [pl.BlockSpec((tile, height), lambda n: (n, 0))],
        out_specs=[
            pl.BlockSpec((channels // 2, tile), lambda n: (0, jnp.minimum(n, steps - 1))),
            pl.BlockSpec((channels // 2, tile), lambda n: (0, jnp.maximum(n - steps, 0))),
        ],
        out_shape=[jax.ShapeDtypeStruct((channels // 2, units), jnp.float32)] * 2,
        compiler_params=pltpu.CompilerParams(vmem_limit_bytes=grant),
        cost_estimate=light,
        name="mix",
    )(high, high, low, low, weight)


def stack_kernel(count, parts, *refs):
    for out_ref, (top, bottom, left, right) in zip(refs[count:], parts):
        for n, ref in enumerate(refs[:count]):
            out_ref[n * (bottom - top) : (n + 1) * (bottom - top), :] = ref[top:bottom, left:right]


def stack(values, parts):
    shapes = [(len(values) * (bottom - top), right - left) for top, bottom, left, right in parts]
    return pl.pallas_call(
        functools.partial(stack_kernel, len(values), parts),
        grid=(1,),
        in_specs=[pl.BlockSpec(value.shape, lambda n: (0, 0)) for value in values],
        out_specs=[pl.BlockSpec(shape, lambda n: (0, 0)) for shape in shapes],
        out_shape=[jax.ShapeDtypeStruct(shape, jnp.float32) for shape in shapes],
        compiler_params=pltpu.CompilerParams(vmem_limit_bytes=grant),
        cost_estimate=light,
        name="stack",
    )(*values)


def halve_kernel(kept_a, sent_a, kept_b, sent_b, *outs):
    for kept, sent, (top, bottom) in ((kept_a, sent_a, outs[:2]), (kept_b, sent_b, outs[2:])):
        total = kept[...] + sent[...]
        top[...], bottom[...] = total[: total.shape[0] // 2], total[total.shape[0] // 2 :]


def halve(values):
    rows, units = values[0].shape
    tile = tile_of(units)
    column = lambda n: (0, n)
    return pl.pallas_call(
        halve_kernel,
        grid=(units // tile,),
        in_specs=[pl.BlockSpec((rows, tile), column)] * 4,
        out_specs=[pl.BlockSpec((rows // 2, tile), column)] * 4,
        out_shape=[jax.ShapeDtypeStruct((rows // 2, units), jnp.float32)] * 4,
        compiler_params=pltpu.CompilerParams(vmem_limit_bytes=grant),
        cost_estimate=light,
        name="halve",
    )(*values)


def merge_kernel(kept_a, sent_a, kept_b, sent_b, *outs):
    middle = kept_a.shape[1]
    for n, out_ref in enumerate(outs):
        block = slice(n * out_ref.shape[0], (n + 1) * out_ref.shape[0])
        out_ref[:, :middle] = kept_a[block, :] + sent_a[block, :]
        out_ref[:, middle:] = kept_b[block, :] + sent_b[block, :]


def merge(values, deep):
    rows, units = values[0].shape
    shape = rows // deep, 2 * units
    return pl.pallas_call(
        merge_kernel,
        grid=(1,),
        in_specs=[pl.BlockSpec(value.shape, lambda n: (0, 0)) for value in values],
        out_specs=[pl.BlockSpec(shape, lambda n: (0, 0))] * deep,
        out_shape=[jax.ShapeDtypeStruct(shape, jnp.float32)] * deep,
        compiler_params=pltpu.CompilerParams(vmem_limit_bytes=grant),
        cost_estimate=light,
        name="merge",
    )(*values)


def project_kernel(rows, places, weight_ref, *refs):
    pieces, (out_ref, active_high, active_low) = refs[:-3], refs[-3:]
    count = len(pieces) // 2
    middle = pieces[0].shape[1]

    @pl.when(pl.program_id(0) == 0)
    def _():
        for n, piece in enumerate(pieces):
            active_high[n * rows : (n + 1) * rows, :], active_low[n * rows : (n + 1) * rows, :] = halves(piece[...])

    high, low = halves(weight_ref[...].T)
    sums = []
    for part in range(2):
        taken = slice(part * count * rows, (part + 1) * count * rows)
        units = slice(part * middle, (part + 1) * middle)
        product = three_pass((active_high[taken, :], active_low[taken, :]), (high[units, :], low[units, :]))
        sums += [product[n * rows : (n + 1) * rows] for n in range(count)]
    for group in range(out_ref.shape[0] // rows):
        target = slice(group * rows, (group + 1) * rows)
        terms = [value for value, place in zip(sums, places) if place == group]
        out_ref[target, :] = functools.reduce(lambda a, b: a + b, terms)


def project(weight, pieces, places):
    width, units = weight.shape
    rows = pieces[0].shape[0]
    groups = 1 + max(places)
    tile = tile_of(width)
    return pl.pallas_call(
        functools.partial(project_kernel, rows, places),
        grid=(width // tile,),
        in_specs=[pl.BlockSpec((tile, units), lambda n: (n, 0))]
        + [pl.BlockSpec(piece.shape, lambda n: (0, 0)) for piece in pieces],
        out_specs=pl.BlockSpec((groups * rows, tile), lambda n: (0, n)),
        out_shape=jax.ShapeDtypeStruct((groups * rows, width), jnp.float32),
        scratch_shapes=[pltpu.VMEM((len(pieces) * rows, units // 2), jnp.bfloat16)] * 2,
        compiler_params=pltpu.CompilerParams(vmem_limit_bytes=grant),
        cost_estimate=light,
        name="project",
    )(weight, *pieces)


def norm_two_kernel(grid, rows, per_core, parts, place_ref, gain_ref, fields_ref, *refs):
    terms, (mixed_ref, high_ref, low_ref) = refs[:-3], refs[-3:]
    starts = block_starts(grid, place_ref, rows, per_core)
    gain = jnp.concatenate([gain_ref[pl.ds(start, rows), :] for start in starts], axis=0)
    total = [ref[...] for ref in terms[:parts]]
    for n in range(parts, len(terms)):
        total[n % parts] = total[n % parts] + terms[n][...]
    mixed = fields_ref[...] + join(total)
    mixed_ref[...] = mixed
    high_ref[...], low_ref[...] = halves(column_norm(mixed, gain))


def norm_two(grid, place, gain, fields, terms, parts, per_core):
    channels, width = fields.shape
    tile = tile_of(width)
    whole = pl.BlockSpec((channels, tile), lambda n, place: (0, n))
    return pl.pallas_call(
        functools.partial(norm_two_kernel, grid, channels // grid.tok, per_core, parts),
        grid_spec=pltpu.PrefetchScalarGridSpec(
            num_scalar_prefetch=1,
            grid=(width // tile,),
            in_specs=[pl.BlockSpec((channels, 1), lambda n, place: (0, 0)), whole]
            + [pl.BlockSpec((term.shape[0], tile), lambda n, place: (0, n)) for term in terms],
            out_specs=[whole] * 3,
        ),
        out_shape=[
            jax.ShapeDtypeStruct((channels, width), kind) for kind in (jnp.float32, jnp.bfloat16, jnp.bfloat16)
        ],
        compiler_params=pltpu.CompilerParams(vmem_limit_bytes=grant),
        cost_estimate=light,
        name="norm_two",
    )(place, gain, fields, *terms)


def expand_kernel(groups, count, high_ref, low_ref, bias_ref, *refs):
    pieces, (out_high, out_low, weight_high, weight_low) = refs[:count], refs[count:]

    @pl.when(pl.program_id(0) == 0)
    def _():
        column = 0
        for group in groups:
            value = jnp.concatenate([pieces[n][start : start + rows, :] for n, start, rows in group], axis=0)
            columns = slice(column, column + value.shape[0])
            weight_high[:, columns], weight_low[:, columns] = halves(value.T)
            column += value.shape[0]

    total = three_pass((weight_high[...], weight_low[...]), (high_ref[...], low_ref[...])) + bias_ref[...]
    active = 0.5 * total * (1.0 + lax.erf(total * 0.7071067811865476))
    out_high[...], out_low[...] = halves(active)


def expand(high, low, bias, pieces, groups):
    depth, width = high.shape
    units = pieces[0].shape[1]
    tile = tile_of(width)
    normed = pl.BlockSpec((depth, tile), lambda n: (0, n))
    return pl.pallas_call(
        functools.partial(expand_kernel, groups, len(pieces)),
        grid=(width // tile,),
        in_specs=[normed, normed, pl.BlockSpec((units, 1), lambda n: (0, 0))]
        + [pl.BlockSpec(piece.shape, lambda n: (0, 0)) for piece in pieces],
        out_specs=[pl.BlockSpec((units, tile), lambda n: (0, n))] * 2,
        out_shape=[jax.ShapeDtypeStruct((units, width), jnp.bfloat16)] * 2,
        scratch_shapes=[pltpu.VMEM((units, depth), jnp.bfloat16)] * 2,
        compiler_params=pltpu.CompilerParams(vmem_limit_bytes=grant),
        cost_estimate=light,
        name="expand",
    )(high, low, bias, *pieces)


def reduce_kernel(groups, count, first, spread, *refs):
    if spread:
        place_ref, refs = refs[0], refs[1:]
    (high_ref, low_ref), pieces, refs = refs[:2], refs[2 : 2 + count], refs[2 + count :]
    if not first:
        start_ref, refs = refs[0], refs[1:]
    if spread:
        mixed_ref, refs = refs[0], refs[1:]
    outs, (weight_high, weight_low) = refs[:-2], refs[-2:]

    @pl.when(pl.program_id(0) == 0)
    def _():
        row = 0
        for group in groups:
            for piece, start, rows in group:
                high, low = halves(pieces[piece][start : start + rows, :])
                weight_high[row : row + rows, :] = high
                weight_low[row : row + rows, :] = low
                row += rows

    total = three_pass((weight_high[...], weight_low[...]), (high_ref[...], low_ref[...]))
    if not first:
        total = start_ref[...] + total
    if not spread:
        outs[0][...] = total
        return
    grid, rows, per_core = spread
    for n, start in enumerate(block_starts(grid, place_ref, rows, per_core)):
        block = slice(n * rows, (n + 1) * rows)
        row = pl.multiple_of(lax.rem(start, per_core * rows), rows)
        step = lax.div(start, per_core * rows)
        for core, out_ref in enumerate(outs):
            value = total[block] + mixed_ref[block, :] if core == 0 else total[block]

            @pl.when(step == core)
            def _():
                out_ref[pl.ds(row, rows), :] = value


def reduce(high, low, pieces, groups, start, spread=None, place=None, mixed=None):
    units, width = high.shape
    rows = sum(piece.shape[0] for piece in pieces)
    tile = tile_of(width)
    hidden = pl.BlockSpec((units, tile), lambda n, *_: (0, n))
    total = pl.BlockSpec((rows, tile), lambda n, *_: (0, n))
    first = start is None
    outs = spread[0].ch if spread else 1
    return pl.pallas_call(
        functools.partial(reduce_kernel, groups, len(pieces), first, spread),
        grid_spec=pltpu.PrefetchScalarGridSpec(
            num_scalar_prefetch=1 if spread else 0,
            grid=(width // tile,),
            in_specs=[hidden, hidden]
            + [pl.BlockSpec(piece.shape, lambda n, *_: (0, 0)) for piece in pieces]
            + [total] * ((not first) + (mixed is not None)),
            out_specs=[pl.BlockSpec((rows // outs, tile), lambda n, *_: (0, n))] * outs,
            scratch_shapes=[pltpu.VMEM((rows, units), jnp.bfloat16)] * 2,
        ),
        out_shape=[jax.ShapeDtypeStruct((rows // outs, width), jnp.float32)] * outs,
        compiler_params=pltpu.CompilerParams(vmem_limit_bytes=grant),
        cost_estimate=light,
        name="reduce",
    )(*([place] if spread else []), high, low, *pieces, *([] if first else [start]), *([mixed] if spread else []))


def finish_kernel(*refs):
    total = refs[0][...]
    for ref in refs[1:-1]:
        total = total + ref[...]
    refs[-1][...] = total.T


def finish(values):
    channels, width = values[0].shape
    tile = tile_of(width)
    return pl.pallas_call(
        finish_kernel,
        grid=(width // tile,),
        in_specs=[pl.BlockSpec((channels, tile), lambda n: (0, n))] * len(values),
        out_specs=pl.BlockSpec((tile, channels), lambda n: (n, 0)),
        out_shape=jax.ShapeDtypeStruct((width, channels), jnp.float32),
        compiler_params=pltpu.CompilerParams(vmem_limit_bytes=grant),
        cost_estimate=light,
        name="finish",
    )(*values)


def join(values, axis=0):
    return jnp.concatenate(list(values), axis=axis)


def shards(
    grid,
    fields,
    gain_one,
    tok_in_weight,
    tok_in_bias,
    tok_out_weight,
    gain_two,
    ch_in_weight,
    ch_in_bias,
    ch_out_weight,
):
    ch, deep, move = grid.ch, grid.deep, grid.move
    width = fields.shape[1]
    rows = ch * width // grid.tok
    per_core = width // rows
    core = lax.axis_index("ch")
    z, y, x = grid.place(lax.axis_index("tok"))
    place = jnp.stack([z, y, x, core]).astype(jnp.int32)

    def keys(outer, inner, low=0, high=2):
        fixed = {"y": range(2), "x": range(2), "z": range(deep), outer: range(low, high)}
        names = outer + inner
        return [
            (dict(zip(names, key))["z"], dict(zip(names, key))["y"], dict(zip(names, key))["x"])
            for key in ((o, m, i) for o in fixed[names[0]] for m in fixed[names[1]] for i in fixed[names[2]])
        ]

    def lone(outer, inner):
        return [keys(outer, inner, n, n + 1) for n in range(deep if outer == "z" else 2)]

    whole = keys("z", "yx", 0, deep)
    corner = {(b, a): [key for key in whole if key[1:] == (b, a)] for b in range(2) for a in range(2)}
    y_last = grid.segments([corner[0, 0], corner[0, 1], corner[1, 0], corner[1, 1]], rows)
    x_last = grid.segments([corner[0, 0], corner[1, 0], corner[0, 1], corner[1, 1]], rows)
    z_after_xy = grid.segments(lone("z", "yx"), rows)
    z_after_yx = grid.segments(lone("z", "xy"), rows)

    units = ch_in_weight.shape[1]
    ends = [units * n // 3 for n in range(4)]
    spans = list(zip(ends, ends[1:]))
    out_rows = ch_out_weight.T

    others = [grid.to_core(fields, ch - step) for step in range(1, ch)]
    pair_gain = jnp.stack([gain_one, gain_two])
    gains = join([pair_gain] + [grid.to_core(pair_gain, ch - step) for step in range(1, ch)], 1).T
    own = join([ch_in_weight[:, : ends[2]], out_rows[:, : ends[2]]])
    in_last, out_last = ch_in_weight[:, ends[2] :], out_rows[:, ends[2] :]
    ring = [move(own, dz=1)]
    in_step, out_step = move(in_last, dx=1), move(out_last, dy=1)
    full, high, low = norm_one(grid, place, gains[:, :1], [fields] + others, per_core)
    high, in_step, out_step = fence(high, in_step, out_step)
    in_last, out_last = join([in_last, in_step]), join([out_last, out_step])
    in_step, out_step = move(in_last, dy=1), move(out_last, dx=1)

    middle = tok_in_weight.shape[0] // 2
    quarter = deep * rows
    sent_a, sent_b = mix(high, low, tok_in_weight, False)
    sent_a, sent_b, ring[0], in_step, out_step = fence(sent_a, sent_b, ring[0], in_step, out_step)
    sent_a, sent_b = move(sent_a, dx=1), move(sent_b, dy=1)
    ring.append(move(ring[0], dz=1))
    kept_a, kept_b = mix(high, low, tok_in_weight, True)
    biases = [ch_in_bias[a:b, None] for a, b in spans]
    in_last, out_last = join([in_last, in_step]), join([out_last, out_step])
    sent_a, sent_b, kept_a, kept_b, in_last, out_last, ring[1], *biases = fence(
        sent_a, sent_b, kept_a, kept_b, in_last, out_last, ring[1], *biases
    )
    kept_a, sent_a, kept_b, sent_b = halve([kept_a, sent_a, kept_b, sent_b])
    sent_a, sent_b = move(sent_a, dy=1), move(sent_b, dx=1)
    for _ in range(2, deep - 1):
        ring.append(move(ring[-1], dz=1))
    sent_a, sent_b, ring[-1] = fence(sent_a, sent_b, ring[-1])

    partial = merge([kept_a, sent_a, kept_b, sent_b], deep)
    total = partial[deep - 1]
    for step in range(2, deep + 1):
        total = move(total, dz=1) + partial[deep - step]
    lines = stack(grid.line(own, ring), [(r, r + rows, a, b) for r in (0, rows) for a, b in spans[:2]])
    first, second = [[line] for line in lines[:2]], [[line] for line in lines[2:]]
    first_step = [move(first[0][0], dx=1), move(first[1][0], dy=1)]
    activated = jax.nn.gelu(total + tok_in_bias[None, :], approximate=False)

    activated, *lines = fence(activated, first[0][0], first[1][0], *first_step)
    first = [[lines[0], lines[2]], [lines[1], lines[3]]]
    ring = []
    for step in range(1, deep):
        ring.append(move(ring[-1] if ring else activated, dz=1))
    first_step = [move(value, dy=1) for value in first[0]] + [move(value, dx=1) for value in first[1]]
    ring[-1], in_last, *first_step = fence(ring[-1], in_last, *first_step)
    first = [first[0] + first_step[:2], first[1] + first_step[2:]]

    active_a, active_b = stack(grid.line(activated, ring), [(0, rows, 0, middle), (0, rows, middle, 2 * middle)])
    arrived = [move(active_a, dy=1), move(active_a, dx=1), move(active_b, dx=1), move(active_b, dy=1)]
    in_ring = [move(in_last, dz=1)]
    in_ring[0], *arrived = fence(in_ring[0], *arrived)
    last_a, last_b = move(arrived[0], dx=1), move(arrived[2], dy=1)
    in_ring.append(move(in_ring[0], dz=1))
    most = project(tok_out_weight, [active_a, *arrived[:2], active_b, *arrived[2:]], (0, 2, 1, 0, 1, 2))
    last_a, last_b, in_ring[1], most = fence(last_a, last_b, in_ring[1], most)

    for _ in range(2, deep - 1):
        in_ring.append(move(in_ring[-1], dz=1))
    second_step = [move(second[0][0], dy=1), move(second[1][0], dx=1)]
    most = [most] + [grid.to_core(most, step) for step in range(1, ch)]
    least = project(tok_out_weight, [last_a, last_b], (0, 0))
    least = [least] + [grid.to_core(least, step) for step in range(1, ch)]
    terms = [part for pair in zip(most, least) for part in pair]
    mixed, high, low = norm_two(grid, place, gains[:, 1:], full, terms, 2, per_core)

    hidden = [expand(high, low, biases[0], first[0], y_last)]
    hidden_high, out_last, in_ring[-1], *second_step = fence(hidden[0][0], out_last, in_ring[-1], *second_step)
    hidden[0] = hidden_high, hidden[0][1]
    second = [line + [step] for line, step in zip(second, second_step)]
    second_step = [move(value, dx=1) for value in second[0]] + [move(value, dy=1) for value in second[1]]
    out_ring = [move(out_last, dz=1)]
    hidden += [
        expand(high, low, biases[1], first[1], x_last),
        expand(high, low, biases[2], grid.line(in_last, in_ring), z_after_xy),
    ]
    fenced = fence(hidden[1][0], hidden[2][0], out_ring[0])
    hidden[1:] = [(fenced[0], hidden[1][1]), (fenced[1], hidden[2][1])]
    out_ring = [fenced[2], move(fenced[2], dz=1)]
    (result,) = reduce(*hidden[0], second[0] + second_step[:2], x_last, None)
    result, out_ring[1], *second_step[2:] = fence(result, out_ring[1], *second_step[2:])
    for _ in range(2, deep - 1):
        out_ring.append(move(out_ring[-1], dz=1))
    (result,) = reduce(*hidden[1], second[1] + second_step[2:], y_last, result)
    spread = grid, rows, per_core
    parts = reduce(*hidden[2], grid.line(out_last, out_ring), z_after_yx, result, spread, place, mixed)
    return finish([parts[0]] + [grid.to_core(part, step) for step, part in enumerate(parts) if step])


def solution(mesh):
    grid = Grid(mesh.shape["tok"], mesh.shape["ch"])
    in_specs = (
        P("tok", "ch"),
        P("ch"),
        P("ch", "tok"),
        P("ch"),
        P("tok", "ch"),
        P("ch"),
        P("tok", "ch"),
        P("ch"),
        P("ch", "tok"),
    )

    def block(*arrays):
        return shards(grid, *arrays)

    return jax.shard_map(block, mesh=mesh, in_specs=in_specs, out_specs=P("tok", "ch"), check_vma=False)
```

```python
import functools

import jax
import jax.numpy as jnp
from jax import lax
from jax.experimental import pallas as pl
from jax.experimental.pallas import tpu as pltpu
from jax.sharding import PartitionSpec as P

epsilon = 1e-05
grant = 255 * 1024 * 256


light = pl.CostEstimate(flops=0, bytes_accessed=0, transcendentals=0)


def empty_kernel(*refs):
    pass


def fence(*values):
    anywhere = [pl.BlockSpec(memory_space=pl.ANY)] * len(values)
    return pl.pallas_call(
        empty_kernel,
        in_specs=anywhere,
        out_specs=anywhere,
        out_shape=[jax.ShapeDtypeStruct(value.shape, value.dtype) for value in values],
        input_output_aliases={n: n for n in range(len(values))},
        compiler_params=pltpu.CompilerParams(vmem_limit_bytes=grant),
        cost_estimate=light,
        name="fence",
    )(*values)


def halves(value):
    high = value.astype(jnp.bfloat16)
    return high, (value - high.astype(jnp.float32)).astype(jnp.bfloat16)


def three_pass(left, right):
    def product(a, b):
        return jnp.dot(a, b, preferred_element_type=jnp.float32)

    return product(left[0], right[0]) + (product(left[0], right[1]) + product(left[1], right[0]))


def column_norm(values, gain):
    centre = jnp.mean(values, axis=0, keepdims=True)
    centred = values - centre
    spread = jnp.mean(centred * centred, axis=0, keepdims=True)
    return centred * lax.rsqrt(spread + epsilon) * gain


def tile_of(size):
    return 256 if size % 256 == 0 else size


class Grid:
    def __init__(self, tok, ch):
        self.tok, self.ch, self.deep = tok, ch, tok // 4
        self.keys = [(c, b, a) for b in range(2) for a in range(2) for c in range(self.deep)]

    def index(self, z, y, x):
        return (z * 2 + y) * 2 + x

    def place(self, chip):
        return chip // 4, chip // 2 % 2, chip % 2

    def move(self, value, dz=0, dy=0, dx=0):
        pairs = []
        for chip in range(self.tok):
            z, y, x = self.place(chip)
            pairs.append((chip, self.index((z + dz) % self.deep, (y + dy) % 2, (x + dx) % 2)))
        return lax.ppermute(value, "tok", pairs)

    def to_core(self, value, step):
        return lax.ppermute(value, "ch", [(core, (core + step) % self.ch) for core in range(self.ch)])

    def line(self, own, arrived):
        return [own] + list(arrived)[::-1]

    def segments(self, orders, rows):
        where = {key: (n, m * rows) for n, order in enumerate(orders) for m, key in enumerate(order)}
        groups = []
        for start in range(0, len(self.keys), self.deep):
            group = []
            for key in self.keys[start : start + self.deep]:
                piece, row = where[key]
                if group and group[-1][0] == piece and group[-1][1] + group[-1][2] == row:
                    group[-1] = piece, group[-1][1], group[-1][2] + rows
                else:
                    group.append((piece, row, rows))
            groups.append(group)
        return groups


def block_starts(grid, place_ref, rows, per_core):
    z, y, x, core = (place_ref[n] for n in range(4))
    starts = []
    for c, b, a in grid.keys:
        owner = grid.index(lax.rem(z + c, grid.deep), lax.rem(y + b, 2), lax.rem(x + a, 2))
        half = lax.rem(lax.div(owner, per_core) + grid.ch - core, grid.ch)
        starts.append(pl.multiple_of((half * per_core + lax.rem(owner, per_core)) * rows, rows))
    return starts


def norm_one_kernel(grid, rows, per_core, place_ref, gain_ref, *refs):
    sources, (fields_ref, high_ref, low_ref, raw, ready) = refs[: grid.ch], refs[grid.ch :]
    values = jnp.concatenate([ref[...].T for ref in sources], axis=0)
    raw[...] = values
    ready[...] = column_norm(values, gain_ref[...])
    for n, start in enumerate(block_starts(grid, place_ref, rows, per_core)):
        target = slice(n * rows, (n + 1) * rows)
        fields_ref[target, :] = raw[pl.ds(start, rows), :]
        high_ref[target, :], low_ref[target, :] = halves(ready[pl.ds(start, rows), :])


def norm_one(grid, place, gain, sources, per_core):
    height, width = sources[0].shape
    channels = width * grid.ch
    tile = tile_of(height)
    whole = pl.BlockSpec((channels, tile), lambda n, place: (0, n))
    return pl.pallas_call(
        functools.partial(norm_one_kernel, grid, channels // grid.tok, per_core),
        grid_spec=pltpu.PrefetchScalarGridSpec(
            num_scalar_prefetch=1,
            grid=(height // tile,),
            in_specs=[pl.BlockSpec((channels, 1), lambda n, place: (0, 0))]
            + [pl.BlockSpec((tile, width), lambda n, place: (n, 0))] * grid.ch,
            out_specs=[whole] * 3,
            scratch_shapes=[pltpu.VMEM((channels, tile), jnp.float32)] * 2,
        ),
        out_shape=[
            jax.ShapeDtypeStruct((channels, height), kind) for kind in (jnp.float32, jnp.bfloat16, jnp.bfloat16)
        ],
        compiler_params=pltpu.CompilerParams(vmem_limit_bytes=grant),
        cost_estimate=light,
        name="norm_one",
    )(place, gain, *sources)


def mix_kernel(steps, high_one, high_two, low_one, low_two, weight_ref, out_a, out_b):
    normed = join([high_one[...], high_two[...]]), join([low_one[...], low_two[...]])
    product = three_pass(normed, halves(weight_ref[...].T))
    part = pl.program_id(0) // steps

    @pl.when(part == 0)
    def _():
        out_a[...] = product

    @pl.when(part == 1)
    def _():
        out_b[...] = product


def mix(high, low, weight, kept):
    channels, height = high.shape
    units = weight.shape[0] // 2
    tile = tile_of(units)
    steps = units // tile
    if kept:
        quarters = lambda n: 0, lambda n: 2 - n // steps
    else:
        quarters = lambda n: 1 + n // steps, lambda n: 3
    picked = [pl.BlockSpec((channels // 4, height), lambda n, q=q: (q(n), 0)) for q in quarters]
    return pl.pallas_call(
        functools.partial(mix_kernel, steps),
        grid=(2 * steps,),
        in_specs=picked * 2 + [pl.BlockSpec((tile, height), lambda n: (n, 0))],
        out_specs=[
            pl.BlockSpec((channels // 2, tile), lambda n: (0, jnp.minimum(n, steps - 1))),
            pl.BlockSpec((channels // 2, tile), lambda n: (0, jnp.maximum(n - steps, 0))),
        ],
        out_shape=[jax.ShapeDtypeStruct((channels // 2, units), jnp.float32)] * 2,
        compiler_params=pltpu.CompilerParams(vmem_limit_bytes=grant),
        cost_estimate=light,
        name="mix",
    )(high, high, low, low, weight)


def stack_kernel(count, outs, *refs):
    for out_ref, parts in zip(refs[count:], outs):
        row = 0
        for top, bottom, left, right in parts:
            for ref in refs[:count]:
                out_ref[row : row + bottom - top, :] = ref[top:bottom, left:right]
                row += bottom - top


def stack(values, *outs):
    shapes = [
        (len(values) * sum(bottom - top for top, bottom, _, _ in parts), parts[0][3] - parts[0][2]) for parts in outs
    ]
    return pl.pallas_call(
        functools.partial(stack_kernel, len(values), outs),
        grid=(1,),
        in_specs=[pl.BlockSpec(value.shape, lambda n: (0, 0)) for value in values],
        out_specs=[pl.BlockSpec(shape, lambda n: (0, 0)) for shape in shapes],
        out_shape=[jax.ShapeDtypeStruct(shape, jnp.float32) for shape in shapes],
        compiler_params=pltpu.CompilerParams(vmem_limit_bytes=grant),
        cost_estimate=light,
        name="stack",
    )(*values)


def halve_kernel(kept_a, sent_a, kept_b, sent_b, *outs):
    for kept, sent, (top, bottom) in ((kept_a, sent_a, outs[:2]), (kept_b, sent_b, outs[2:])):
        total = kept[...] + sent[...]
        top[...], bottom[...] = total[: total.shape[0] // 2], total[total.shape[0] // 2 :]


def halve(values):
    rows, units = values[0].shape
    tile = tile_of(units)
    column = lambda n: (0, n)
    return pl.pallas_call(
        halve_kernel,
        grid=(units // tile,),
        in_specs=[pl.BlockSpec((rows, tile), column)] * 4,
        out_specs=[pl.BlockSpec((rows // 2, tile), column)] * 4,
        out_shape=[jax.ShapeDtypeStruct((rows // 2, units), jnp.float32)] * 4,
        compiler_params=pltpu.CompilerParams(vmem_limit_bytes=grant),
        cost_estimate=light,
        name="halve",
    )(*values)


def merge_kernel(kept_a, sent_a, kept_b, sent_b, *outs):
    middle = kept_a.shape[1]
    for n, out_ref in enumerate(outs):
        block = slice(n * out_ref.shape[0], (n + 1) * out_ref.shape[0])
        out_ref[:, :middle] = kept_a[block, :] + sent_a[block, :]
        out_ref[:, middle:] = kept_b[block, :] + sent_b[block, :]


def merge(values, deep):
    rows, units = values[0].shape
    shape = rows // deep, 2 * units
    return pl.pallas_call(
        merge_kernel,
        grid=(1,),
        in_specs=[pl.BlockSpec(value.shape, lambda n: (0, 0)) for value in values],
        out_specs=[pl.BlockSpec(shape, lambda n: (0, 0))] * deep,
        out_shape=[jax.ShapeDtypeStruct(shape, jnp.float32)] * deep,
        compiler_params=pltpu.CompilerParams(vmem_limit_bytes=grant),
        cost_estimate=light,
        name="merge",
    )(*values)


def project_kernel(rows, places, weight_ref, *refs):
    pieces, (out_ref, active_high, active_low) = refs[:-3], refs[-3:]
    count = len(pieces) // 2
    middle = pieces[0].shape[1]

    @pl.when(pl.program_id(0) == 0)
    def _():
        for n, piece in enumerate(pieces):
            active_high[n * rows : (n + 1) * rows, :], active_low[n * rows : (n + 1) * rows, :] = halves(piece[...])

    high, low = halves(weight_ref[...].T)
    sums = []
    for part in range(2):
        taken = slice(part * count * rows, (part + 1) * count * rows)
        units = slice(part * middle, (part + 1) * middle)
        product = three_pass((active_high[taken, :], active_low[taken, :]), (high[units, :], low[units, :]))
        sums += [product[n * rows : (n + 1) * rows] for n in range(count)]
    for group in range(out_ref.shape[0] // rows):
        target = slice(group * rows, (group + 1) * rows)
        terms = [value for value, place in zip(sums, places) if place == group]
        out_ref[target, :] = functools.reduce(lambda a, b: a + b, terms)


def project(weight, pieces, places):
    width, units = weight.shape
    rows = pieces[0].shape[0]
    groups = 1 + max(places)
    tile = tile_of(width)
    return pl.pallas_call(
        functools.partial(project_kernel, rows, places),
        grid=(width // tile,),
        in_specs=[pl.BlockSpec((tile, units), lambda n: (n, 0))]
        + [pl.BlockSpec(piece.shape, lambda n: (0, 0)) for piece in pieces],
        out_specs=pl.BlockSpec((groups * rows, tile), lambda n: (0, n)),
        out_shape=jax.ShapeDtypeStruct((groups * rows, width), jnp.float32),
        scratch_shapes=[pltpu.VMEM((len(pieces) * rows, units // 2), jnp.bfloat16)] * 2,
        compiler_params=pltpu.CompilerParams(vmem_limit_bytes=grant),
        cost_estimate=light,
        name="project",
    )(weight, *pieces)


def norm_two_kernel(grid, rows, per_core, parts, place_ref, gain_ref, fields_ref, *refs):
    terms, (mixed_ref, high_ref, low_ref) = refs[:-3], refs[-3:]
    starts = block_starts(grid, place_ref, rows, per_core)
    gain = jnp.concatenate([gain_ref[pl.ds(start, rows), :] for start in starts], axis=0)
    total = [ref[...] for ref in terms[:parts]]
    for n in range(parts, len(terms)):
        total[n % parts] = total[n % parts] + terms[n][...]
    mixed = fields_ref[...] + join(total)
    mixed_ref[...] = mixed
    high_ref[...], low_ref[...] = halves(column_norm(mixed, gain))


def norm_two(grid, place, gain, fields, terms, parts, per_core):
    channels, width = fields.shape
    tile = tile_of(width)
    whole = pl.BlockSpec((channels, tile), lambda n, place: (0, n))
    return pl.pallas_call(
        functools.partial(norm_two_kernel, grid, channels // grid.tok, per_core, parts),
        grid_spec=pltpu.PrefetchScalarGridSpec(
            num_scalar_prefetch=1,
            grid=(width // tile,),
            in_specs=[pl.BlockSpec((channels, 1), lambda n, place: (0, 0)), whole]
            + [pl.BlockSpec((term.shape[0], tile), lambda n, place: (0, n)) for term in terms],
            out_specs=[whole] * 3,
        ),
        out_shape=[
            jax.ShapeDtypeStruct((channels, width), kind) for kind in (jnp.float32, jnp.bfloat16, jnp.bfloat16)
        ],
        compiler_params=pltpu.CompilerParams(vmem_limit_bytes=grant),
        cost_estimate=light,
        name="norm_two",
    )(place, gain, fields, *terms)


def expand_kernel(groups, count, high_ref, low_ref, bias_ref, *refs):
    pieces, (out_high, out_low, weight_high, weight_low) = refs[:count], refs[count:]

    @pl.when(pl.program_id(0) == 0)
    def _():
        column = 0
        for group in groups:
            value = jnp.concatenate([pieces[n][start : start + rows, :] for n, start, rows in group], axis=0)
            columns = slice(column, column + value.shape[0])
            weight_high[:, columns], weight_low[:, columns] = halves(value.T)
            column += value.shape[0]

    units = out_high.shape[0]
    tile = tile_of(units)
    for row in range(0, units, tile):
        taken = slice(row, row + tile)
        total = three_pass((weight_high[taken, :], weight_low[taken, :]), (high_ref[...], low_ref[...]))
        total = total + bias_ref[taken, :]
        active = 0.5 * total * (1.0 + lax.erf(total * 0.7071067811865476))
        out_high[taken, :], out_low[taken, :] = halves(active)


def expand(high, low, bias, pieces, groups):
    depth, width = high.shape
    units = pieces[0].shape[1]
    tile = tile_of(width)
    normed = pl.BlockSpec((depth, tile), lambda n: (0, n))
    return pl.pallas_call(
        functools.partial(expand_kernel, groups, len(pieces)),
        grid=(width // tile,),
        in_specs=[normed, normed, pl.BlockSpec((units, 1), lambda n: (0, 0))]
        + [pl.BlockSpec(piece.shape, lambda n: (0, 0)) for piece in pieces],
        out_specs=[pl.BlockSpec((units, tile), lambda n: (0, n))] * 2,
        out_shape=[jax.ShapeDtypeStruct((units, width), jnp.bfloat16)] * 2,
        scratch_shapes=[pltpu.VMEM((units, depth), jnp.bfloat16)] * 2,
        compiler_params=pltpu.CompilerParams(vmem_limit_bytes=grant),
        cost_estimate=light,
        name="expand",
    )(high, low, bias, *pieces)


def reduce_kernel(groups, count, first, spread, *refs):
    if spread:
        place_ref, refs = refs[0], refs[1:]
    (high_ref, low_ref), pieces, refs = refs[:2], refs[2 : 2 + count], refs[2 + count :]
    if not first:
        start_ref, refs = refs[0], refs[1:]
    if spread:
        mixed_ref, refs = refs[0], refs[1:]
    outs, (weight_high, weight_low) = refs[:-2], refs[-2:]

    @pl.when(pl.program_id(0) == 0)
    def _():
        row = 0
        for group in groups:
            for piece, start, rows in group:
                high, low = halves(pieces[piece][start : start + rows, :])
                weight_high[row : row + rows, :] = high
                weight_low[row : row + rows, :] = low
                row += rows

    total = three_pass((weight_high[...], weight_low[...]), (high_ref[...], low_ref[...]))
    if not first:
        total = start_ref[...] + total
    if not spread:
        outs[0][...] = total
        return
    grid, rows, per_core = spread
    for n, start in enumerate(block_starts(grid, place_ref, rows, per_core)):
        block = slice(n * rows, (n + 1) * rows)
        row = pl.multiple_of(lax.rem(start, per_core * rows), rows)
        step = lax.div(start, per_core * rows)
        for core, out_ref in enumerate(outs):
            value = total[block] + mixed_ref[block, :] if core == 0 else total[block]

            @pl.when(step == core)
            def _():
                out_ref[pl.ds(row, rows), :] = value


def reduce(high, low, pieces, groups, start, spread=None, place=None, mixed=None):
    units, width = high.shape
    rows = sum(piece.shape[0] for piece in pieces)
    tile = tile_of(width)
    hidden = pl.BlockSpec((units, tile), lambda n, *_: (0, n))
    total = pl.BlockSpec((rows, tile), lambda n, *_: (0, n))
    first = start is None
    outs = spread[0].ch if spread else 1
    return pl.pallas_call(
        functools.partial(reduce_kernel, groups, len(pieces), first, spread),
        grid_spec=pltpu.PrefetchScalarGridSpec(
            num_scalar_prefetch=1 if spread else 0,
            grid=(width // tile,),
            in_specs=[hidden, hidden]
            + [pl.BlockSpec(piece.shape, lambda n, *_: (0, 0)) for piece in pieces]
            + [total] * ((not first) + (mixed is not None)),
            out_specs=[pl.BlockSpec((rows // outs, tile), lambda n, *_: (0, n))] * outs,
            scratch_shapes=[pltpu.VMEM((rows, units), jnp.bfloat16)] * 2,
        ),
        out_shape=[jax.ShapeDtypeStruct((rows // outs, width), jnp.float32)] * outs,
        compiler_params=pltpu.CompilerParams(vmem_limit_bytes=grant),
        cost_estimate=light,
        name="reduce",
    )(*([place] if spread else []), high, low, *pieces, *([] if first else [start]), *([mixed] if spread else []))


def finish_kernel(*refs):
    total = refs[0][...]
    for ref in refs[1:-1]:
        total = total + ref[...]
    refs[-1][...] = total.T


def finish(values):
    channels, width = values[0].shape
    tile = tile_of(width)
    return pl.pallas_call(
        finish_kernel,
        grid=(width // tile,),
        in_specs=[pl.BlockSpec((channels, tile), lambda n: (0, n))] * len(values),
        out_specs=pl.BlockSpec((tile, channels), lambda n: (n, 0)),
        out_shape=jax.ShapeDtypeStruct((width, channels), jnp.float32),
        compiler_params=pltpu.CompilerParams(vmem_limit_bytes=grant),
        cost_estimate=light,
        name="finish",
    )(*values)


def join(values, axis=0):
    return jnp.concatenate(list(values), axis=axis)


def shards(
    grid,
    fields,
    gain_one,
    tok_in_weight,
    tok_in_bias,
    tok_out_weight,
    gain_two,
    ch_in_weight,
    ch_in_bias,
    ch_out_weight,
):
    ch, deep, move = grid.ch, grid.deep, grid.move
    width = fields.shape[1]
    rows = ch * width // grid.tok
    per_core = width // rows
    core = lax.axis_index("ch")
    z, y, x = grid.place(lax.axis_index("tok"))
    place = jnp.stack([z, y, x, core]).astype(jnp.int32)

    def keys(outer, inner, low=0, high=2):
        fixed = {"y": range(2), "x": range(2), "z": range(deep), outer: range(low, high)}
        names = outer + inner
        return [
            (dict(zip(names, key))["z"], dict(zip(names, key))["y"], dict(zip(names, key))["x"])
            for key in ((o, m, i) for o in fixed[names[0]] for m in fixed[names[1]] for i in fixed[names[2]])
        ]

    def lone(outer, inner):
        return [keys(outer, inner, n, n + 1) for n in range(deep if outer == "z" else 2)]

    whole = keys("z", "yx", 0, deep)
    corner = {(b, a): [key for key in whole if key[1:] == (b, a)] for b in range(2) for a in range(2)}
    y_last = grid.segments([corner[0, 0], corner[0, 1], corner[1, 0], corner[1, 1]], rows)
    x_last = grid.segments([corner[0, 0], corner[1, 0], corner[0, 1], corner[1, 1]], rows)
    y_last_pair = grid.segments([corner[0, 0] + corner[0, 1], corner[1, 0] + corner[1, 1]], rows)
    x_last_pair = grid.segments([corner[0, 0] + corner[1, 0], corner[0, 1] + corner[1, 1]], rows)
    z_after_xy = grid.segments(lone("z", "yx"), rows)
    z_after_yx = grid.segments(lone("z", "xy"), rows)

    units = ch_in_weight.shape[1]
    ends = [units * n // 3 for n in range(4)]
    spans = list(zip(ends, ends[1:]))
    out_rows = ch_out_weight.T

    others = [grid.to_core(fields, ch - step) for step in range(1, ch)]
    pair_gain = jnp.stack([gain_one, gain_two])
    gains = join([pair_gain] + [grid.to_core(pair_gain, ch - step) for step in range(1, ch)], 1).T
    own = join([ch_in_weight[:, : ends[2]], out_rows[:, : ends[2]]])
    in_last, out_last = ch_in_weight[:, ends[2] :], out_rows[:, ends[2] :]
    ring = [move(own, dz=1)]
    in_step, out_step = move(in_last, dx=1), move(out_last, dy=1)
    full, high, low = norm_one(grid, place, gains[:, :1], [fields] + others, per_core)
    high, in_step, out_step = fence(high, in_step, out_step)
    in_last, out_last = join([in_last, in_step]), join([out_last, out_step])
    in_step, out_step = move(in_last, dy=1), move(out_last, dx=1)

    middle = tok_in_weight.shape[0] // 2
    quarter = deep * rows
    sent_a, sent_b = mix(high, low, tok_in_weight, False)
    sent_a, sent_b, ring[0], in_step, out_step = fence(sent_a, sent_b, ring[0], in_step, out_step)
    sent_a, sent_b = move(sent_a, dx=1), move(sent_b, dy=1)
    ring.append(move(ring[0], dz=1))
    kept_a, kept_b = mix(high, low, tok_in_weight, True)
    biases = [ch_in_bias[a:b, None] for a, b in spans]
    in_last, out_last = join([in_last, in_step]), join([out_last, out_step])
    sent_a, sent_b, kept_a, kept_b, in_last, out_last, ring[1], *biases = fence(
        sent_a, sent_b, kept_a, kept_b, in_last, out_last, ring[1], *biases
    )
    kept_a, sent_a, kept_b, sent_b = halve([kept_a, sent_a, kept_b, sent_b])
    sent_a, sent_b = move(sent_a, dy=1), move(sent_b, dx=1)
    for _ in range(2, deep - 1):
        ring.append(move(ring[-1], dz=1))
    sent_a, sent_b, ring[-1] = fence(sent_a, sent_b, ring[-1])

    partial = merge([kept_a, sent_a, kept_b, sent_b], deep)
    total = partial[deep - 1]
    for step in range(2, deep + 1):
        total = move(total, dz=1) + partial[deep - step]
    (in_a, in_b), (out_a, out_b) = [[(top, top + rows, a, b) for a, b in spans[:2]] for top in (0, rows)]
    pack_x, pack_y, line_a, line_b = stack(grid.line(own, ring), [in_a, out_b], [in_b, out_a], [in_a], [in_b])
    got_x, got_y = move(pack_x, dx=1), move(pack_y, dy=1)
    in_ring = [move(in_last, dz=1)]
    activated = jax.nn.gelu(total + tok_in_bias[None, :], approximate=False)

    activated, line_a, line_b, got_x, got_y, in_ring[0] = fence(activated, line_a, line_b, got_x, got_y, in_ring[0])
    ring = []
    for step in range(1, deep):
        ring.append(move(ring[-1] if ring else activated, dz=1))
    step_a, step_b = got_x[:quarter], got_y[:quarter]
    first_step = [move(line_a, dy=1), move(step_a, dy=1), move(line_b, dx=1), move(step_b, dx=1)]
    ring[-1], *first_step = fence(ring[-1], *first_step)
    first = [[line_a, step_a, *first_step[:2]], [line_b, step_b, *first_step[2:]]]

    active_a, active_b = stack(grid.line(activated, ring), [(0, rows, 0, middle)], [(0, rows, middle, 2 * middle)])
    lower = quarter, 2 * quarter, 0, ends[1]
    second = [stack([pack_y, got_y], [lower])[0], stack([pack_x, got_x], [lower])[0]]
    arrived = [move(active_a, dy=1), move(active_a, dx=1), move(active_b, dx=1), move(active_b, dy=1)]
    in_ring.append(move(in_ring[0], dz=1))
    in_ring[1], second[0], second[1], *arrived = fence(in_ring[1], *second, *arrived)
    last_a, last_b = move(arrived[0], dx=1), move(arrived[2], dy=1)
    for _ in range(2, deep - 1):
        in_ring.append(move(in_ring[-1], dz=1))
    most = project(tok_out_weight, [active_a, *arrived[:2], active_b, *arrived[2:]], (0, 2, 1, 0, 1, 2))
    last_a, last_b, in_ring[-1], most = fence(last_a, last_b, in_ring[-1], most)

    second_step = [move(second[0], dx=1), move(second[1], dy=1)]
    out_ring = [move(out_last, dz=1)]
    most = [most] + [grid.to_core(most, step) for step in range(1, ch)]
    least = project(tok_out_weight, [last_a, last_b], (0, 0))
    least = [least] + [grid.to_core(least, step) for step in range(1, ch)]
    terms = [part for pair in zip(most, least) for part in pair]
    mixed, high, low = norm_two(grid, place, gains[:, 1:], full, terms, 2, per_core)

    hidden = [expand(high, low, biases[0], first[0], y_last)]
    hidden_high, out_ring[0] = fence(hidden[0][0], out_ring[0])
    hidden[0] = hidden_high, hidden[0][1]
    out_ring.append(move(out_ring[0], dz=1))
    hidden += [
        expand(high, low, biases[1], first[1], x_last),
        expand(high, low, biases[2], grid.line(in_last, in_ring), z_after_xy),
    ]
    fenced = fence(hidden[1][0], hidden[2][0], out_ring[1], *second_step)
    hidden[1:] = [(fenced[0], hidden[1][1]), (fenced[1], hidden[2][1])]
    out_ring[1], *second_step = fenced[2:]
    for _ in range(2, deep - 1):
        out_ring.append(move(out_ring[-1], dz=1))
    (result,) = reduce(*hidden[0], [second[0], second_step[0]], x_last_pair, None)
    (result,) = reduce(*hidden[1], [second[1], second_step[1]], y_last_pair, result)
    spread = grid, rows, per_core
    parts = reduce(*hidden[2], grid.line(out_last, out_ring), z_after_yx, result, spread, place, mixed)
    return finish([parts[0]] + [grid.to_core(part, step) for step, part in enumerate(parts) if step])


def solution(mesh):
    grid = Grid(mesh.shape["tok"], mesh.shape["ch"])
    in_specs = (
        P("tok", "ch"),
        P("ch"),
        P("ch", "tok"),
        P("ch"),
        P("tok", "ch"),
        P("ch"),
        P("tok", "ch"),
        P("ch"),
        P("ch", "tok"),
    )

    def block(*arrays):
        return shards(grid, *arrays)

    return jax.shard_map(block, mesh=mesh, in_specs=in_specs, out_specs=P("tok", "ch"), check_vma=False)
```

```python
import functools

import jax
import jax.numpy as jnp
from jax import lax
from jax.experimental import pallas as pl
from jax.experimental.pallas import tpu as pltpu
from jax.sharding import PartitionSpec as P

epsilon = 1e-05
grant = 255 * 1024 * 256


light = pl.CostEstimate(flops=0, bytes_accessed=0, transcendentals=0)


def empty_kernel(*refs):
    pass


def fence(*values):
    anywhere = [pl.BlockSpec(memory_space=pl.ANY)] * len(values)
    return pl.pallas_call(
        empty_kernel,
        in_specs=anywhere,
        out_specs=anywhere,
        out_shape=[jax.ShapeDtypeStruct(value.shape, value.dtype) for value in values],
        input_output_aliases={n: n for n in range(len(values))},
        compiler_params=pltpu.CompilerParams(vmem_limit_bytes=grant),
        cost_estimate=light,
        name="fence",
    )(*values)


def halves(value):
    high = value.astype(jnp.bfloat16)
    return high, (value - high.astype(jnp.float32)).astype(jnp.bfloat16)


def three_pass(left, right):
    def product(a, b):
        return jnp.dot(a, b, preferred_element_type=jnp.float32)

    return product(left[0], right[0]) + (product(left[0], right[1]) + product(left[1], right[0]))


def column_norm(values, gain):
    centre = jnp.mean(values, axis=0, keepdims=True)
    centred = values - centre
    spread = jnp.mean(centred * centred, axis=0, keepdims=True)
    return centred * lax.rsqrt(spread + epsilon) * gain


def tile_of(size):
    return 256 if size % 256 == 0 else size


class Grid:
    def __init__(self, tok, ch):
        self.tok, self.ch, self.deep = tok, ch, tok // 4
        self.keys = [(c, b, a) for b in range(2) for a in range(2) for c in range(self.deep)]

    def index(self, z, y, x):
        return (z * 2 + y) * 2 + x

    def place(self, chip):
        return chip // 4, chip // 2 % 2, chip % 2

    def move(self, value, dz=0, dy=0, dx=0):
        pairs = []
        for chip in range(self.tok):
            z, y, x = self.place(chip)
            pairs.append((chip, self.index((z + dz) % self.deep, (y + dy) % 2, (x + dx) % 2)))
        return lax.ppermute(value, "tok", pairs)

    def to_core(self, value, step):
        return lax.ppermute(value, "ch", [(core, (core + step) % self.ch) for core in range(self.ch)])

    def line(self, own, arrived):
        return [own] + list(arrived)[::-1]

    def segments(self, orders, rows):
        where = {key: (n, m * rows) for n, order in enumerate(orders) for m, key in enumerate(order)}
        groups = []
        for start in range(0, len(self.keys), self.deep):
            group = []
            for key in self.keys[start : start + self.deep]:
                piece, row = where[key]
                if group and group[-1][0] == piece and group[-1][1] + group[-1][2] == row:
                    group[-1] = piece, group[-1][1], group[-1][2] + rows
                else:
                    group.append((piece, row, rows))
            groups.append(group)
        return groups


def block_starts(grid, place_ref, rows, per_core):
    z, y, x, core = (place_ref[n] for n in range(4))
    starts = []
    for c, b, a in grid.keys:
        owner = grid.index(lax.rem(z + c, grid.deep), lax.rem(y + b, 2), lax.rem(x + a, 2))
        half = lax.rem(lax.div(owner, per_core) + grid.ch - core, grid.ch)
        starts.append(pl.multiple_of((half * per_core + lax.rem(owner, per_core)) * rows, rows))
    return starts


def norm_one_kernel(grid, rows, per_core, place_ref, gain_ref, *refs):
    sources, (fields_ref, high_ref, low_ref, raw, ready) = refs[: grid.ch], refs[grid.ch :]
    values = jnp.concatenate([ref[...].T for ref in sources], axis=0)
    raw[...] = values
    ready[...] = column_norm(values, gain_ref[...])
    for n, start in enumerate(block_starts(grid, place_ref, rows, per_core)):
        target = slice(n * rows, (n + 1) * rows)
        fields_ref[target, :] = raw[pl.ds(start, rows), :]
        high_ref[target, :], low_ref[target, :] = halves(ready[pl.ds(start, rows), :])


def norm_one(grid, place, gain, sources, per_core):
    height, width = sources[0].shape
    channels = width * grid.ch
    tile = tile_of(height)
    whole = pl.BlockSpec((channels, tile), lambda n, place: (0, n))
    return pl.pallas_call(
        functools.partial(norm_one_kernel, grid, channels // grid.tok, per_core),
        grid_spec=pltpu.PrefetchScalarGridSpec(
            num_scalar_prefetch=1,
            grid=(height // tile,),
            in_specs=[pl.BlockSpec((channels, 1), lambda n, place: (0, 0))]
            + [pl.BlockSpec((tile, width), lambda n, place: (n, 0))] * grid.ch,
            out_specs=[whole] * 3,
            scratch_shapes=[pltpu.VMEM((channels, tile), jnp.float32)] * 2,
        ),
        out_shape=[
            jax.ShapeDtypeStruct((channels, height), kind) for kind in (jnp.float32, jnp.bfloat16, jnp.bfloat16)
        ],
        compiler_params=pltpu.CompilerParams(vmem_limit_bytes=grant),
        cost_estimate=light,
        name="norm_one",
    )(place, gain, *sources)


def mix_kernel(steps, high_one, high_two, low_one, low_two, weight_ref, out_a, out_b):
    normed = join([high_one[...], high_two[...]]), join([low_one[...], low_two[...]])
    product = three_pass(normed, halves(weight_ref[...].T))
    part = pl.program_id(0) // steps

    @pl.when(part == 0)
    def _():
        out_a[...] = product

    @pl.when(part == 1)
    def _():
        out_b[...] = product


def mix(high, low, weight, kept):
    channels, height = high.shape
    units = weight.shape[0] // 2
    tile = tile_of(units)
    steps = units // tile
    if kept:
        quarters = lambda n: 0, lambda n: 2 - n // steps
    else:
        quarters = lambda n: 1 + n // steps, lambda n: 3
    picked = [pl.BlockSpec((channels // 4, height), lambda n, q=q: (q(n), 0)) for q in quarters]
    return pl.pallas_call(
        functools.partial(mix_kernel, steps),
        grid=(2 * steps,),
        in_specs=picked * 2 + [pl.BlockSpec((tile, height), lambda n: (n, 0))],
        out_specs=[
            pl.BlockSpec((channels // 2, tile), lambda n: (0, jnp.minimum(n, steps - 1))),
            pl.BlockSpec((channels // 2, tile), lambda n: (0, jnp.maximum(n - steps, 0))),
        ],
        out_shape=[jax.ShapeDtypeStruct((channels // 2, units), jnp.float32)] * 2,
        compiler_params=pltpu.CompilerParams(vmem_limit_bytes=grant),
        cost_estimate=light,
        name="mix",
    )(high, high, low, low, weight)


def stack_kernel(count, outs, *refs):
    for out_ref, parts in zip(refs[count:], outs):
        row = 0
        for top, bottom, left, right in parts:
            for ref in refs[:count]:
                out_ref[row : row + bottom - top, :] = ref[top:bottom, left:right]
                row += bottom - top


def stack(values, *outs):
    shapes = [
        (len(values) * sum(bottom - top for top, bottom, _, _ in parts), parts[0][3] - parts[0][2]) for parts in outs
    ]
    return pl.pallas_call(
        functools.partial(stack_kernel, len(values), outs),
        grid=(1,),
        in_specs=[pl.BlockSpec(value.shape, lambda n: (0, 0)) for value in values],
        out_specs=[pl.BlockSpec(shape, lambda n: (0, 0)) for shape in shapes],
        out_shape=[jax.ShapeDtypeStruct(shape, jnp.float32) for shape in shapes],
        compiler_params=pltpu.CompilerParams(vmem_limit_bytes=grant),
        cost_estimate=light,
        name="stack",
    )(*values)


def halve_kernel(kept_a, sent_a, kept_b, sent_b, out_a, out_b):
    out_a[...] = kept_a[...] + sent_a[...]
    out_b[...] = kept_b[...] + sent_b[...]


def halve(values):
    rows, units = values[0].shape
    tile = tile_of(units)
    return pl.pallas_call(
        halve_kernel,
        grid=(units // tile,),
        in_specs=[pl.BlockSpec((rows // 2, tile), lambda n: (1, n))] * 4,
        out_specs=[pl.BlockSpec((rows // 2, tile), lambda n: (0, n))] * 2,
        out_shape=[jax.ShapeDtypeStruct((rows // 2, units), jnp.float32)] * 2,
        compiler_params=pltpu.CompilerParams(vmem_limit_bytes=grant),
        cost_estimate=light,
        name="halve",
    )(*values)


def merge_kernel(*refs):
    (kept_a, sent_a, last_a, kept_b, sent_b, last_b), outs = refs[:6], refs[6:]
    middle = kept_a.shape[1]
    for n, out_ref in enumerate(outs):
        block = slice(n * out_ref.shape[0], (n + 1) * out_ref.shape[0])
        out_ref[:, :middle] = kept_a[block, :] + sent_a[block, :] + last_a[block, :]
        out_ref[:, middle:] = kept_b[block, :] + sent_b[block, :] + last_b[block, :]


def merge(values, deep):
    rows, units = values[2].shape
    shape = rows // deep, 2 * units
    return pl.pallas_call(
        merge_kernel,
        grid=(1,),
        in_specs=[pl.BlockSpec((rows, units), lambda n: (0, 0))] * 6,
        out_specs=[pl.BlockSpec(shape, lambda n: (0, 0))] * deep,
        out_shape=[jax.ShapeDtypeStruct(shape, jnp.float32)] * deep,
        compiler_params=pltpu.CompilerParams(vmem_limit_bytes=grant),
        cost_estimate=light,
        name="merge",
    )(*values)


def project_kernel(rows, places, high, low, *refs):
    pieces, (out_ref, active_high, active_low) = refs[:-3], refs[-3:]
    count = len(pieces) // 2
    middle = pieces[0].shape[1]

    @pl.when(pl.program_id(0) == 0)
    def _():
        for n, piece in enumerate(pieces):
            active_high[n * rows : (n + 1) * rows, :], active_low[n * rows : (n + 1) * rows, :] = halves(piece[...])

    sums = []
    for part in range(2):
        taken = slice(part * count * rows, (part + 1) * count * rows)
        units = slice(part * middle, (part + 1) * middle)
        product = three_pass((active_high[taken, :], active_low[taken, :]), (high[units, :], low[units, :]))
        sums += [product[n * rows : (n + 1) * rows] for n in range(count)]
    for group in range(out_ref.shape[0] // rows):
        target = slice(group * rows, (group + 1) * rows)
        terms = [value for value, place in zip(sums, places) if place == group]
        out_ref[target, :] = functools.reduce(lambda a, b: a + b, terms)


def project(high, low, pieces, places):
    units, width = high.shape
    rows = pieces[0].shape[0]
    groups = 1 + max(places)
    tile = tile_of(width)
    return pl.pallas_call(
        functools.partial(project_kernel, rows, places),
        grid=(width // tile,),
        in_specs=[pl.BlockSpec((units, tile), lambda n: (0, n))] * 2
        + [pl.BlockSpec(piece.shape, lambda n: (0, 0)) for piece in pieces],
        out_specs=pl.BlockSpec((groups * rows, tile), lambda n: (0, n)),
        out_shape=jax.ShapeDtypeStruct((groups * rows, width), jnp.float32),
        scratch_shapes=[pltpu.VMEM((len(pieces) * rows, units // 2), jnp.bfloat16)] * 2,
        compiler_params=pltpu.CompilerParams(vmem_limit_bytes=grant),
        cost_estimate=light,
        name="project",
    )(high, low, *pieces)


def norm_two_kernel(grid, rows, per_core, parts, place_ref, gain_ref, fields_ref, *refs):
    terms, (mixed_ref, high_ref, low_ref) = refs[:-3], refs[-3:]
    starts = block_starts(grid, place_ref, rows, per_core)
    gain = jnp.concatenate([gain_ref[pl.ds(start, rows), :] for start in starts], axis=0)
    total = [ref[...] for ref in terms[:parts]]
    for n in range(parts, len(terms)):
        total[n % parts] = total[n % parts] + terms[n][...]
    mixed = fields_ref[...] + join(total)
    mixed_ref[...] = mixed
    high_ref[...], low_ref[...] = halves(column_norm(mixed, gain))


def norm_two(grid, place, gain, fields, terms, parts, per_core):
    channels, width = fields.shape
    tile = tile_of(width)
    whole = pl.BlockSpec((channels, tile), lambda n, place: (0, n))
    return pl.pallas_call(
        functools.partial(norm_two_kernel, grid, channels // grid.tok, per_core, parts),
        grid_spec=pltpu.PrefetchScalarGridSpec(
            num_scalar_prefetch=1,
            grid=(width // tile,),
            in_specs=[pl.BlockSpec((channels, 1), lambda n, place: (0, 0)), whole]
            + [pl.BlockSpec((term.shape[0], tile), lambda n, place: (0, n)) for term in terms],
            out_specs=[whole] * 3,
        ),
        out_shape=[
            jax.ShapeDtypeStruct((channels, width), kind) for kind in (jnp.float32, jnp.bfloat16, jnp.bfloat16)
        ],
        compiler_params=pltpu.CompilerParams(vmem_limit_bytes=grant),
        cost_estimate=light,
        name="norm_two",
    )(place, gain, fields, *terms)


def prepare_kernel(groups, count, *refs):
    pieces, (high_ref, low_ref) = refs[:count], refs[count:]
    column = 0
    for group in groups:
        value = join([pieces[n][start : start + rows, :] for n, start, rows in group])
        columns = slice(column, column + value.shape[0])
        high_ref[:, columns], low_ref[:, columns] = halves(value.T)
        column += value.shape[0]


def prepare(pieces, groups):
    shape = pieces[0].shape[1], sum(piece.shape[0] for piece in pieces)
    return pl.pallas_call(
        functools.partial(prepare_kernel, groups, len(pieces)),
        grid=(1,),
        in_specs=[pl.BlockSpec(piece.shape, lambda n: (0, 0)) for piece in pieces],
        out_specs=[pl.BlockSpec(shape, lambda n: (0, 0))] * 2,
        out_shape=[jax.ShapeDtypeStruct(shape, jnp.bfloat16)] * 2,
        compiler_params=pltpu.CompilerParams(vmem_limit_bytes=grant),
        cost_estimate=light,
        name="prepare",
    )(*pieces)


def expand_kernel(groups, count, high_ref, low_ref, bias_ref, *refs):
    pieces, outs, weights = refs[:count], refs[count : count + 2], refs[count + 2 :]
    if weights:

        @pl.when(pl.program_id(0) == 0)
        def _():
            prepare_kernel(groups, count, *pieces, *weights)

    else:
        weights = pieces
    total = three_pass((weights[0][...], weights[1][...]), (high_ref[...], low_ref[...])) + bias_ref[...]
    active = 0.5 * total * (1.0 + lax.erf(total * 0.7071067811865476))
    outs[0][...], outs[1][...] = halves(active)


def expand(high, low, bias, pieces, groups=None):
    depth, width = high.shape
    units = bias.shape[0]
    tile = tile_of(width)
    normed = pl.BlockSpec((depth, tile), lambda n: (0, n))
    return pl.pallas_call(
        functools.partial(expand_kernel, groups, len(pieces)),
        grid=(width // tile,),
        in_specs=[normed, normed, pl.BlockSpec((units, 1), lambda n: (0, 0))]
        + [pl.BlockSpec(piece.shape, lambda n: (0, 0)) for piece in pieces],
        out_specs=[pl.BlockSpec((units, tile), lambda n: (0, n))] * 2,
        out_shape=[jax.ShapeDtypeStruct((units, width), jnp.bfloat16)] * 2,
        scratch_shapes=[pltpu.VMEM((units, depth), jnp.bfloat16)] * (2 if groups else 0),
        compiler_params=pltpu.CompilerParams(vmem_limit_bytes=grant),
        cost_estimate=light,
        name="expand",
    )(high, low, bias, *pieces)


def reduce_kernel(orders, counts, first, spread, *refs):
    if spread:
        place_ref, refs = refs[0], refs[1:]
    hidden, refs = refs[: 2 * len(counts)], refs[2 * len(counts) :]
    pieces, refs = refs[: sum(counts)], refs[sum(counts) :]
    if not first:
        start_ref, refs = refs[0], refs[1:]
    if spread:
        mixed_ref, refs = refs[0], refs[1:]
    outs, (weight_high, weight_low) = refs[:-2], refs[-2:]
    width = pieces[0].shape[1]

    @pl.when(pl.program_id(0) == 0)
    def _():
        for chunk, groups in enumerate(orders):
            offset, row = sum(counts[:chunk]), 0
            columns = slice(chunk * width, (chunk + 1) * width)
            for group in groups:
                for piece, start, rows in group:
                    high, low = halves(pieces[offset + piece][start : start + rows, :])
                    weight_high[row : row + rows, columns] = high
                    weight_low[row : row + rows, columns] = low
                    row += rows

    total = None
    for chunk in range(len(counts)):
        columns = slice(chunk * width, (chunk + 1) * width)
        high_ref, low_ref = hidden[2 * chunk : 2 * chunk + 2]
        term = three_pass((weight_high[:, columns], weight_low[:, columns]), (high_ref[...], low_ref[...]))
        total = term if total is None else total + term
    if not first:
        total = start_ref[...] + total
    if not spread:
        outs[0][...] = total
        return
    grid, rows, per_core = spread
    for n, start in enumerate(block_starts(grid, place_ref, rows, per_core)):
        block = slice(n * rows, (n + 1) * rows)
        row = pl.multiple_of(lax.rem(start, per_core * rows), rows)
        step = lax.div(start, per_core * rows)
        for core, out_ref in enumerate(outs):
            value = total[block] + mixed_ref[block, :] if core == 0 else total[block]

            @pl.when(step == core)
            def _():
                out_ref[pl.ds(row, rows), :] = value


def reduce(chunks, start=None, spread=None, place=None, mixed=None):
    hidden = [half for chunk in chunks for half in chunk[0]]
    pieces = [piece for chunk in chunks for piece in chunk[1]]
    units, width = hidden[0].shape
    rows = sum(piece.shape[0] for piece in chunks[0][1])
    tile = tile_of(width)
    total = pl.BlockSpec((rows, tile), lambda n, *_: (0, n))
    first = start is None
    outs = spread[0].ch if spread else 1
    return pl.pallas_call(
        functools.partial(
            reduce_kernel, [chunk[2] for chunk in chunks], [len(chunk[1]) for chunk in chunks], first, spread
        ),
        grid_spec=pltpu.PrefetchScalarGridSpec(
            num_scalar_prefetch=1 if spread else 0,
            grid=(width // tile,),
            in_specs=[pl.BlockSpec((units, tile), lambda n, *_: (0, n))] * len(hidden)
            + [pl.BlockSpec(piece.shape, lambda n, *_: (0, 0)) for piece in pieces]
            + [total] * ((not first) + (mixed is not None)),
            out_specs=[pl.BlockSpec((rows // outs, tile), lambda n, *_: (0, n))] * outs,
            scratch_shapes=[pltpu.VMEM((rows, len(chunks) * units), jnp.bfloat16)] * 2,
        ),
        out_shape=[jax.ShapeDtypeStruct((rows // outs, width), jnp.float32)] * outs,
        compiler_params=pltpu.CompilerParams(vmem_limit_bytes=grant),
        cost_estimate=light,
        name="reduce",
    )(*([place] if spread else []), *hidden, *pieces, *([] if first else [start]), *([mixed] if spread else []))


def finish_kernel(*refs):
    total = refs[0][...]
    for ref in refs[1:-1]:
        total = total + ref[...]
    refs[-1][...] = total.T


def finish(values):
    channels, width = values[0].shape
    tile = tile_of(width)
    return pl.pallas_call(
        finish_kernel,
        grid=(width // tile,),
        in_specs=[pl.BlockSpec((channels, tile), lambda n: (0, n))] * len(values),
        out_specs=pl.BlockSpec((tile, channels), lambda n: (n, 0)),
        out_shape=jax.ShapeDtypeStruct((width, channels), jnp.float32),
        compiler_params=pltpu.CompilerParams(vmem_limit_bytes=grant),
        cost_estimate=light,
        name="finish",
    )(*values)


def cut_kernel(in_ref, out_ref, own_ref, in_last, out_last):
    rows, units = in_ref.shape[0], own_ref.shape[1]
    own_ref[:rows, :], own_ref[rows:, :] = in_ref[:, :units], out_ref[:, :units]
    in_last[...], out_last[...] = in_ref[:, units:], out_ref[:, units:]


def cut(in_rows, out_rows, units):
    rows, total = in_rows.shape
    whole = pl.BlockSpec((rows, total), lambda n: (0, 0))
    shapes = [(2 * rows, units)] + [(rows, total - units)] * 2
    return pl.pallas_call(
        cut_kernel,
        grid=(1,),
        in_specs=[whole, whole],
        out_specs=[pl.BlockSpec(shape, lambda n: (0, 0)) for shape in shapes],
        out_shape=[jax.ShapeDtypeStruct(shape, jnp.float32) for shape in shapes],
        compiler_params=pltpu.CompilerParams(vmem_limit_bytes=grant),
        cost_estimate=light,
        name="cut",
    )(in_rows, out_rows)


def join(values, axis=0):
    return jnp.concatenate(list(values), axis=axis)


def shards(
    grid,
    fields,
    gain_one,
    tok_in_weight,
    tok_in_bias,
    tok_out_weight,
    gain_two,
    ch_in_weight,
    ch_in_bias,
    ch_out_weight,
):
    ch, deep, move = grid.ch, grid.deep, grid.move
    width = fields.shape[1]
    rows = ch * width // grid.tok
    per_core = width // rows
    core = lax.axis_index("ch")
    z, y, x = grid.place(lax.axis_index("tok"))
    place = jnp.stack([z, y, x, core]).astype(jnp.int32)

    def keys(outer, inner, low=0, high=2):
        fixed = {"y": range(2), "x": range(2), "z": range(deep), outer: range(low, high)}
        names = outer + inner
        return [
            (dict(zip(names, key))["z"], dict(zip(names, key))["y"], dict(zip(names, key))["x"])
            for key in ((o, m, i) for o in fixed[names[0]] for m in fixed[names[1]] for i in fixed[names[2]])
        ]

    def lone(outer, inner):
        return [keys(outer, inner, n, n + 1) for n in range(deep if outer == "z" else 2)]

    whole = keys("z", "yx", 0, deep)
    corner = {(b, a): [key for key in whole if key[1:] == (b, a)] for b in range(2) for a in range(2)}
    y_last = grid.segments([corner[0, 0], corner[0, 1], corner[1, 0], corner[1, 1]], rows)
    x_last = grid.segments([corner[0, 0], corner[1, 0], corner[0, 1], corner[1, 1]], rows)
    y_last_pair = grid.segments([corner[0, 0] + corner[0, 1], corner[1, 0] + corner[1, 1]], rows)
    x_last_pair = grid.segments([corner[0, 0] + corner[1, 0], corner[0, 1] + corner[1, 1]], rows)
    z_after_xy = grid.segments(lone("z", "yx"), rows)
    z_after_yx = grid.segments(lone("z", "xy"), rows)

    units = ch_in_weight.shape[1]
    ends = [units * n // 3 for n in range(4)]
    spans = list(zip(ends, ends[1:]))
    out_rows = ch_out_weight.T

    others = [grid.to_core(fields, ch - step) for step in range(1, ch)]
    pair_gain = jnp.stack([gain_one, gain_two])
    gains = join([pair_gain] + [grid.to_core(pair_gain, ch - step) for step in range(1, ch)], 1).T
    own, in_last, out_last = cut(ch_in_weight, out_rows, ends[2])
    ring = [move(own, dz=1)]
    in_step, out_step = move(in_last, dx=1), move(out_last, dy=1)
    full, high, low = norm_one(grid, place, gains[:, :1], [fields] + others, per_core)
    high, in_step, out_step = fence(high, in_step, out_step)
    in_last, out_last = join([in_last, in_step]), join([out_last, out_step])
    in_step, out_step = move(in_last, dy=1), move(out_last, dx=1)

    middle = tok_in_weight.shape[0] // 2
    quarter = deep * rows
    sent_a, sent_b = mix(high, low, tok_in_weight, False)
    sent_a, sent_b, ring[0], in_step, out_step = fence(sent_a, sent_b, ring[0], in_step, out_step)
    sent_a, sent_b = move(sent_a, dx=1), move(sent_b, dy=1)
    ring.append(move(ring[0], dz=1))
    kept_a, kept_b = mix(high, low, tok_in_weight, True)
    biases = [ch_in_bias[a:b, None] for a, b in spans]
    in_last, out_last = join([in_last, in_step]), join([out_last, out_step])
    sent_a, sent_b, kept_a, kept_b, in_last, out_last, ring[1], *biases = fence(
        sent_a, sent_b, kept_a, kept_b, in_last, out_last, ring[1], *biases
    )
    last_a, last_b = halve([kept_a, sent_a, kept_b, sent_b])
    last_a, last_b = move(last_a, dy=1), move(last_b, dx=1)
    for _ in range(2, deep - 1):
        ring.append(move(ring[-1], dz=1))
    last_a, last_b, ring[-1] = fence(last_a, last_b, ring[-1])

    partial = merge([kept_a, sent_a, last_a, kept_b, sent_b, last_b], deep)
    total = partial[deep - 1]
    for step in range(2, deep + 1):
        total = move(total, dz=1) + partial[deep - step]
    (in_a, in_b), (out_a, out_b) = [[(top, top + rows, a, b) for a, b in spans[:2]] for top in (0, rows)]
    pack_x, pack_y, line_a, line_b = stack(grid.line(own, ring), [in_a, out_b], [in_b, out_a], [in_a], [in_b])
    got_x, got_y = move(pack_x, dx=1), move(pack_y, dy=1)
    in_ring = [move(in_last, dz=1)]
    activated = jax.nn.gelu(total + tok_in_bias[None, :], approximate=False)

    activated, line_a, line_b, got_x, got_y, in_ring[0] = fence(activated, line_a, line_b, got_x, got_y, in_ring[0])
    ring = []
    for step in range(1, deep):
        ring.append(move(ring[-1] if ring else activated, dz=1))
    step_a, step_b = got_x[:quarter], got_y[:quarter]
    first_step = [move(line_a, dy=1), move(step_a, dy=1), move(line_b, dx=1), move(step_b, dx=1)]
    span = tok_out_weight.shape[0]
    out_high, out_low = prepare([tok_out_weight], [[(0, 0, span)]])
    ring[-1], out_high, out_low, *first_step = fence(ring[-1], out_high, out_low, *first_step)
    first = [
        *prepare([line_a, step_a, *first_step[:2]], y_last),
        *prepare([line_b, step_b, *first_step[2:]], x_last),
    ]

    active_a, active_b = stack(grid.line(activated, ring), [(0, rows, 0, middle)], [(0, rows, middle, 2 * middle)])
    lower = quarter, 2 * quarter, 0, ends[1]
    second = [stack([pack_y, got_y], [lower])[0], stack([pack_x, got_x], [lower])[0]]
    arrived = [move(active_a, dy=1), move(active_a, dx=1), move(active_b, dx=1), move(active_b, dy=1)]
    in_ring.append(move(in_ring[0], dz=1))
    in_ring[1], *fenced = fence(in_ring[1], *second, *first, *arrived)
    second, first, arrived = fenced[:2], (fenced[2:4], fenced[4:6]), fenced[6:]
    last_a, last_b = move(arrived[0], dx=1), move(arrived[2], dy=1)
    for _ in range(2, deep - 1):
        in_ring.append(move(in_ring[-1], dz=1))
    most = project(out_high, out_low, [active_a, *arrived[:2], active_b, *arrived[2:]], (0, 2, 1, 0, 1, 2))
    last_a, last_b, in_ring[-1], most = fence(last_a, last_b, in_ring[-1], most)

    second_step = [move(second[0], dx=1), move(second[1], dy=1)]
    out_ring = [move(out_last, dz=1)]
    most = [most] + [grid.to_core(most, step) for step in range(1, ch)]
    least = project(out_high, out_low, [last_a, last_b], (0, 0))
    least = [least] + [grid.to_core(least, step) for step in range(1, ch)]
    terms = [part for pair in zip(most, least) for part in pair]
    mixed, high, low = norm_two(grid, place, gains[:, 1:], full, terms, 2, per_core)

    hidden = [expand(high, low, biases[0], first[0])]
    hidden_high, out_ring[0] = fence(hidden[0][0], out_ring[0])
    hidden[0] = hidden_high, hidden[0][1]
    out_ring.append(move(out_ring[0], dz=1))
    hidden += [
        expand(high, low, biases[1], first[1]),
        expand(high, low, biases[2], grid.line(in_last, in_ring), z_after_xy),
    ]
    fenced = fence(hidden[1][0], hidden[2][0], out_ring[1], *second_step)
    hidden[1:] = [(fenced[0], hidden[1][1]), (fenced[1], hidden[2][1])]
    out_ring[1], *second_step = fenced[2:]
    for _ in range(2, deep - 1):
        out_ring.append(move(out_ring[-1], dz=1))
    (result,) = reduce(
        [
            (hidden[0], [second[0], second_step[0]], x_last_pair),
            (hidden[1], [second[1], second_step[1]], y_last_pair),
        ]
    )
    spread = grid, rows, per_core
    parts = reduce([(hidden[2], grid.line(out_last, out_ring), z_after_yx)], result, spread, place, mixed)
    return finish([parts[0]] + [grid.to_core(part, step) for step, part in enumerate(parts) if step])


def solution(mesh):
    grid = Grid(mesh.shape["tok"], mesh.shape["ch"])
    in_specs = (
        P("tok", "ch"),
        P("ch"),
        P("ch", "tok"),
        P("ch"),
        P("tok", "ch"),
        P("ch"),
        P("tok", "ch"),
        P("ch"),
        P("ch", "tok"),
    )

    def block(*arrays):
        return shards(grid, *arrays)

    return jax.shard_map(block, mesh=mesh, in_specs=in_specs, out_specs=P("tok", "ch"), check_vma=False)
```

```python
import functools

import jax
import jax.numpy as jnp
from jax import lax
from jax.experimental import pallas as pl
from jax.experimental.pallas import tpu as pltpu
from jax.sharding import PartitionSpec as P

epsilon = 1e-05
grant = 255 * 1024 * 256


light = pl.CostEstimate(flops=0, bytes_accessed=0, transcendentals=0)


def empty_kernel(*refs):
    pass


def fence(*values):
    anywhere = [pl.BlockSpec(memory_space=pl.ANY)] * len(values)
    return pl.pallas_call(
        empty_kernel,
        in_specs=anywhere,
        out_specs=anywhere,
        out_shape=[jax.ShapeDtypeStruct(value.shape, value.dtype) for value in values],
        input_output_aliases={n: n for n in range(len(values))},
        compiler_params=pltpu.CompilerParams(vmem_limit_bytes=grant),
        cost_estimate=light,
        name="fence",
    )(*values)


def halves(value):
    high = value.astype(jnp.bfloat16)
    return high, (value - high.astype(jnp.float32)).astype(jnp.bfloat16)


def three_pass(left, right):
    def product(a, b):
        return jnp.dot(a, b, preferred_element_type=jnp.float32)

    return product(left[0], right[0]) + (product(left[0], right[1]) + product(left[1], right[0]))


def column_norm(values, gain):
    centre = jnp.mean(values, axis=0, keepdims=True)
    centred = values - centre
    spread = jnp.mean(centred * centred, axis=0, keepdims=True)
    return centred * lax.rsqrt(spread + epsilon) * gain


def tile_of(size):
    return 256 if size % 256 == 0 else size


class Grid:
    def __init__(self, tok, ch):
        self.tok, self.ch, self.deep = tok, ch, tok // 4
        self.keys = [(c, b, a) for b in range(2) for a in range(2) for c in range(self.deep)]

    def index(self, z, y, x):
        return (z * 2 + y) * 2 + x

    def place(self, chip):
        return chip // 4, chip // 2 % 2, chip % 2

    def move(self, value, dz=0, dy=0, dx=0):
        pairs = []
        for chip in range(self.tok):
            z, y, x = self.place(chip)
            pairs.append((chip, self.index((z + dz) % self.deep, (y + dy) % 2, (x + dx) % 2)))
        return lax.ppermute(value, "tok", pairs)

    def to_core(self, value, step):
        return lax.ppermute(value, "ch", [(core, (core + step) % self.ch) for core in range(self.ch)])

    def line(self, own, arrived):
        return [own] + list(arrived)[::-1]

    def segments(self, orders, rows):
        where = {key: (n, m * rows) for n, order in enumerate(orders) for m, key in enumerate(order)}
        groups = []
        for start in range(0, len(self.keys), self.deep):
            group = []
            for key in self.keys[start : start + self.deep]:
                piece, row = where[key]
                if group and group[-1][0] == piece and group[-1][1] + group[-1][2] == row:
                    group[-1] = piece, group[-1][1], group[-1][2] + rows
                else:
                    group.append((piece, row, rows))
            groups.append(group)
        return groups


def block_starts(grid, place_ref, rows, per_core):
    z, y, x, core = (place_ref[n] for n in range(4))
    starts = []
    for c, b, a in grid.keys:
        owner = grid.index(lax.rem(z + c, grid.deep), lax.rem(y + b, 2), lax.rem(x + a, 2))
        half = lax.rem(lax.div(owner, per_core) + grid.ch - core, grid.ch)
        starts.append(pl.multiple_of((half * per_core + lax.rem(owner, per_core)) * rows, rows))
    return starts


def norm_one_kernel(grid, rows, per_core, place_ref, gain_ref, *refs):
    sources, (fields_ref, high_ref, low_ref, raw, ready) = refs[: grid.ch], refs[grid.ch :]
    values = jnp.concatenate([ref[...].T for ref in sources], axis=0)
    raw[...] = values
    ready[...] = column_norm(values, gain_ref[...])
    for n, start in enumerate(block_starts(grid, place_ref, rows, per_core)):
        target = slice(n * rows, (n + 1) * rows)
        fields_ref[target, :] = raw[pl.ds(start, rows), :]
        high_ref[target, :], low_ref[target, :] = halves(ready[pl.ds(start, rows), :])


def norm_one(grid, place, gain, sources, per_core):
    height, width = sources[0].shape
    channels = width * grid.ch
    tile = tile_of(height)
    whole = pl.BlockSpec((channels, tile), lambda n, place: (0, n))
    return pl.pallas_call(
        functools.partial(norm_one_kernel, grid, channels // grid.tok, per_core),
        grid_spec=pltpu.PrefetchScalarGridSpec(
            num_scalar_prefetch=1,
            grid=(height // tile,),
            in_specs=[pl.BlockSpec((channels, 1), lambda n, place: (0, 0))]
            + [pl.BlockSpec((tile, width), lambda n, place: (n, 0))] * grid.ch,
            out_specs=[whole] * 3,
            scratch_shapes=[pltpu.VMEM((channels, tile), jnp.float32)] * 2,
        ),
        out_shape=[
            jax.ShapeDtypeStruct((channels, height), kind) for kind in (jnp.float32, jnp.bfloat16, jnp.bfloat16)
        ],
        compiler_params=pltpu.CompilerParams(vmem_limit_bytes=grant),
        cost_estimate=light,
        name="norm_one",
    )(place, gain, *sources)


def mix_kernel(steps, high_one, high_two, low_one, low_two, weight_ref, out_a, out_b):
    normed = join([high_one[...], high_two[...]]), join([low_one[...], low_two[...]])
    product = three_pass(normed, halves(weight_ref[...].T))
    part = pl.program_id(0) // steps

    @pl.when(part == 0)
    def _():
        out_a[...] = product

    @pl.when(part == 1)
    def _():
        out_b[...] = product


def mix(high, low, weight, kept):
    channels, height = high.shape
    units = weight.shape[0] // 2
    tile = tile_of(units)
    steps = units // tile
    if kept:
        quarters = lambda n: 0, lambda n: 2 - n // steps
    else:
        quarters = lambda n: 1 + n // steps, lambda n: 3
    picked = [pl.BlockSpec((channels // 4, height), lambda n, q=q: (q(n), 0)) for q in quarters]
    return pl.pallas_call(
        functools.partial(mix_kernel, steps),
        grid=(2 * steps,),
        in_specs=picked * 2 + [pl.BlockSpec((tile, height), lambda n: (n, 0))],
        out_specs=[
            pl.BlockSpec((channels // 2, tile), lambda n: (0, jnp.minimum(n, steps - 1))),
            pl.BlockSpec((channels // 2, tile), lambda n: (0, jnp.maximum(n - steps, 0))),
        ],
        out_shape=[jax.ShapeDtypeStruct((channels // 2, units), jnp.float32)] * 2,
        compiler_params=pltpu.CompilerParams(vmem_limit_bytes=grant),
        cost_estimate=light,
        name="mix",
    )(high, high, low, low, weight)


def stack_kernel(count, outs, *refs):
    for out_ref, parts in zip(refs[count:], outs):
        row = 0
        for top, bottom, left, right in parts:
            for ref in refs[:count]:
                out_ref[row : row + bottom - top, :] = ref[top:bottom, left:right]
                row += bottom - top


def stack(values, *outs):
    shapes = [
        (len(values) * sum(bottom - top for top, bottom, _, _ in parts), parts[0][3] - parts[0][2]) for parts in outs
    ]
    return pl.pallas_call(
        functools.partial(stack_kernel, len(values), outs),
        grid=(1,),
        in_specs=[pl.BlockSpec(value.shape, lambda n: (0, 0)) for value in values],
        out_specs=[pl.BlockSpec(shape, lambda n: (0, 0)) for shape in shapes],
        out_shape=[jax.ShapeDtypeStruct(shape, jnp.float32) for shape in shapes],
        compiler_params=pltpu.CompilerParams(vmem_limit_bytes=grant),
        cost_estimate=light,
        name="stack",
    )(*values)


def rows_kernel(*refs):
    for ref, out_ref in zip(refs[: len(refs) // 2], refs[len(refs) // 2 :]):
        out_ref[...] = ref[...]


def cut_rows(values, rows):
    units = values[0].shape[1]
    tile = tile_of(units)
    block = pl.BlockSpec((rows, tile), lambda n: (0, n))
    return pl.pallas_call(
        rows_kernel,
        grid=(units // tile,),
        in_specs=[block] * len(values),
        out_specs=[block] * len(values),
        out_shape=[jax.ShapeDtypeStruct((rows, units), jnp.float32)] * len(values),
        compiler_params=pltpu.CompilerParams(vmem_limit_bytes=grant),
        cost_estimate=light,
        name="cut_rows",
    )(*values)


def halve_kernel(kept_a, sent_a, kept_b, sent_b, out_a, out_b):
    out_a[...] = kept_a[...] + sent_a[...]
    out_b[...] = kept_b[...] + sent_b[...]


def halve(values):
    rows, units = values[0].shape
    tile = tile_of(units)
    return pl.pallas_call(
        halve_kernel,
        grid=(units // tile,),
        in_specs=[pl.BlockSpec((rows // 2, tile), lambda n: (1, n))] * 4,
        out_specs=[pl.BlockSpec((rows // 2, tile), lambda n: (0, n))] * 2,
        out_shape=[jax.ShapeDtypeStruct((rows // 2, units), jnp.float32)] * 2,
        compiler_params=pltpu.CompilerParams(vmem_limit_bytes=grant),
        cost_estimate=light,
        name="halve",
    )(*values)


def merge_kernel(*refs):
    (kept_a, sent_a, last_a, kept_b, sent_b, last_b), outs = refs[:6], refs[6:]
    middle = kept_a.shape[1]
    for n, out_ref in enumerate(outs):
        block = slice(n * out_ref.shape[0], (n + 1) * out_ref.shape[0])
        out_ref[:, :middle] = kept_a[block, :] + sent_a[block, :] + last_a[block, :]
        out_ref[:, middle:] = kept_b[block, :] + sent_b[block, :] + last_b[block, :]


def merge(values, deep):
    rows, units = values[2].shape
    shape = rows // deep, 2 * units
    return pl.pallas_call(
        merge_kernel,
        grid=(1,),
        in_specs=[pl.BlockSpec((rows, units), lambda n: (0, 0))] * 6,
        out_specs=[pl.BlockSpec(shape, lambda n: (0, 0))] * deep,
        out_shape=[jax.ShapeDtypeStruct(shape, jnp.float32)] * deep,
        compiler_params=pltpu.CompilerParams(vmem_limit_bytes=grant),
        cost_estimate=light,
        name="merge",
    )(*values)


def project_kernel(rows, places, high, low, *refs):
    pieces, (out_ref, active_high, active_low) = refs[:-3], refs[-3:]
    count = len(pieces) // 2
    middle = pieces[0].shape[1]

    @pl.when(pl.program_id(0) == 0)
    def _():
        for n, piece in enumerate(pieces):
            active_high[n * rows : (n + 1) * rows, :], active_low[n * rows : (n + 1) * rows, :] = halves(piece[...])

    sums = []
    for part in range(2):
        taken = slice(part * count * rows, (part + 1) * count * rows)
        units = slice(part * middle, (part + 1) * middle)
        product = three_pass((active_high[taken, :], active_low[taken, :]), (high[units, :], low[units, :]))
        sums += [product[n * rows : (n + 1) * rows] for n in range(count)]
    for group in range(out_ref.shape[0] // rows):
        target = slice(group * rows, (group + 1) * rows)
        terms = [value for value, place in zip(sums, places) if place == group]
        out_ref[target, :] = functools.reduce(lambda a, b: a + b, terms)


def project(high, low, pieces, places):
    units, width = high.shape
    rows = pieces[0].shape[0]
    groups = 1 + max(places)
    tile = tile_of(width)
    return pl.pallas_call(
        functools.partial(project_kernel, rows, places),
        grid=(width // tile,),
        in_specs=[pl.BlockSpec((units, tile), lambda n: (0, n))] * 2
        + [pl.BlockSpec(piece.shape, lambda n: (0, 0)) for piece in pieces],
        out_specs=pl.BlockSpec((groups * rows, tile), lambda n: (0, n)),
        out_shape=jax.ShapeDtypeStruct((groups * rows, width), jnp.float32),
        scratch_shapes=[pltpu.VMEM((len(pieces) * rows, units // 2), jnp.bfloat16)] * 2,
        compiler_params=pltpu.CompilerParams(vmem_limit_bytes=grant),
        cost_estimate=light,
        name="project",
    )(high, low, *pieces)


def norm_two_kernel(grid, rows, per_core, parts, place_ref, gain_ref, fields_ref, *refs):
    terms, (mixed_ref, high_ref, low_ref) = refs[:-3], refs[-3:]
    starts = block_starts(grid, place_ref, rows, per_core)
    gain = jnp.concatenate([gain_ref[pl.ds(start, rows), :] for start in starts], axis=0)
    total = [ref[...] for ref in terms[:parts]]
    for n in range(parts, len(terms)):
        total[n % parts] = total[n % parts] + terms[n][...]
    mixed = fields_ref[...] + join(total)
    mixed_ref[...] = mixed
    high_ref[...], low_ref[...] = halves(column_norm(mixed, gain))


def norm_two(grid, place, gain, fields, terms, parts, per_core):
    channels, width = fields.shape
    tile = tile_of(width)
    whole = pl.BlockSpec((channels, tile), lambda n, place: (0, n))
    return pl.pallas_call(
        functools.partial(norm_two_kernel, grid, channels // grid.tok, per_core, parts),
        grid_spec=pltpu.PrefetchScalarGridSpec(
            num_scalar_prefetch=1,
            grid=(width // tile,),
            in_specs=[pl.BlockSpec((channels, 1), lambda n, place: (0, 0)), whole]
            + [pl.BlockSpec((term.shape[0], tile), lambda n, place: (0, n)) for term in terms],
            out_specs=[whole] * 3,
        ),
        out_shape=[
            jax.ShapeDtypeStruct((channels, width), kind) for kind in (jnp.float32, jnp.bfloat16, jnp.bfloat16)
        ],
        compiler_params=pltpu.CompilerParams(vmem_limit_bytes=grant),
        cost_estimate=light,
        name="norm_two",
    )(place, gain, fields, *terms)


def prepare_kernel(groups, count, *refs):
    pieces, (high_ref, low_ref) = refs[:count], refs[count:]
    column = 0
    for group in groups:
        value = join([pieces[n][start : start + rows, :] for n, start, rows in group])
        columns = slice(column, column + value.shape[0])
        high_ref[:, columns], low_ref[:, columns] = halves(value.T)
        column += value.shape[0]


def prepare(pieces, groups):
    shape = pieces[0].shape[1], sum(piece.shape[0] for piece in pieces)
    return pl.pallas_call(
        functools.partial(prepare_kernel, groups, len(pieces)),
        grid=(1,),
        in_specs=[pl.BlockSpec(piece.shape, lambda n: (0, 0)) for piece in pieces],
        out_specs=[pl.BlockSpec(shape, lambda n: (0, 0))] * 2,
        out_shape=[jax.ShapeDtypeStruct(shape, jnp.bfloat16)] * 2,
        compiler_params=pltpu.CompilerParams(vmem_limit_bytes=grant),
        cost_estimate=light,
        name="prepare",
    )(*pieces)


def expand_kernel(groups, count, high_ref, low_ref, bias_ref, *refs):
    pieces, outs, weights = refs[:count], refs[count : count + 2], refs[count + 2 :]
    if weights:

        @pl.when(pl.program_id(0) == 0)
        def _():
            prepare_kernel(groups, count, *pieces, *weights)

    else:
        weights = pieces
    total = three_pass((weights[0][...], weights[1][...]), (high_ref[...], low_ref[...])) + bias_ref[...]
    active = 0.5 * total * (1.0 + lax.erf(total * 0.7071067811865476))
    outs[0][...], outs[1][...] = halves(active)


def expand(high, low, bias, pieces, groups=None):
    depth, width = high.shape
    units = bias.shape[0]
    tile = tile_of(width)
    normed = pl.BlockSpec((depth, tile), lambda n: (0, n))
    return pl.pallas_call(
        functools.partial(expand_kernel, groups, len(pieces)),
        grid=(width // tile,),
        in_specs=[normed, normed, pl.BlockSpec((units, 1), lambda n: (0, 0))]
        + [pl.BlockSpec(piece.shape, lambda n: (0, 0)) for piece in pieces],
        out_specs=[pl.BlockSpec((units, tile), lambda n: (0, n))] * 2,
        out_shape=[jax.ShapeDtypeStruct((units, width), jnp.bfloat16)] * 2,
        scratch_shapes=[pltpu.VMEM((units, depth), jnp.bfloat16)] * (2 if groups else 0),
        compiler_params=pltpu.CompilerParams(vmem_limit_bytes=grant),
        cost_estimate=light,
        name="expand",
    )(high, low, bias, *pieces)


def reduce_kernel(orders, counts, first, spread, *refs):
    if spread:
        place_ref, refs = refs[0], refs[1:]
    hidden, refs = refs[: 2 * len(counts)], refs[2 * len(counts) :]
    pieces, refs = refs[: sum(counts)], refs[sum(counts) :]
    if not first:
        start_ref, refs = refs[0], refs[1:]
    if spread:
        mixed_ref, refs = refs[0], refs[1:]
    outs, (weight_high, weight_low) = refs[:-2], refs[-2:]
    width = pieces[0].shape[1]

    @pl.when(pl.program_id(0) == 0)
    def _():
        for chunk, groups in enumerate(orders):
            offset, row = sum(counts[:chunk]), 0
            columns = slice(chunk * width, (chunk + 1) * width)
            for group in groups:
                for piece, start, rows in group:
                    high, low = halves(pieces[offset + piece][start : start + rows, :])
                    weight_high[row : row + rows, columns] = high
                    weight_low[row : row + rows, columns] = low
                    row += rows

    total = None
    for chunk in range(len(counts)):
        columns = slice(chunk * width, (chunk + 1) * width)
        high_ref, low_ref = hidden[2 * chunk : 2 * chunk + 2]
        term = three_pass((weight_high[:, columns], weight_low[:, columns]), (high_ref[...], low_ref[...]))
        total = term if total is None else total + term
    if not first:
        total = start_ref[...] + total
    if not spread:
        outs[0][...] = total
        return
    grid, rows, per_core = spread
    for n, start in enumerate(block_starts(grid, place_ref, rows, per_core)):
        block = slice(n * rows, (n + 1) * rows)
        row = pl.multiple_of(lax.rem(start, per_core * rows), rows)
        step = lax.div(start, per_core * rows)
        for core, out_ref in enumerate(outs):
            value = total[block] + mixed_ref[block, :] if core == 0 else total[block]

            @pl.when(step == core)
            def _():
                out_ref[pl.ds(row, rows), :] = value


def reduce(chunks, start=None, spread=None, place=None, mixed=None):
    hidden = [half for chunk in chunks for half in chunk[0]]
    pieces = [piece for chunk in chunks for piece in chunk[1]]
    units, width = hidden[0].shape
    rows = sum(piece.shape[0] for piece in chunks[0][1])
    tile = tile_of(width)
    total = pl.BlockSpec((rows, tile), lambda n, *_: (0, n))
    first = start is None
    outs = spread[0].ch if spread else 1
    return pl.pallas_call(
        functools.partial(
            reduce_kernel, [chunk[2] for chunk in chunks], [len(chunk[1]) for chunk in chunks], first, spread
        ),
        grid_spec=pltpu.PrefetchScalarGridSpec(
            num_scalar_prefetch=1 if spread else 0,
            grid=(width // tile,),
            in_specs=[pl.BlockSpec((units, tile), lambda n, *_: (0, n))] * len(hidden)
            + [pl.BlockSpec(piece.shape, lambda n, *_: (0, 0)) for piece in pieces]
            + [total] * ((not first) + (mixed is not None)),
            out_specs=[pl.BlockSpec((rows // outs, tile), lambda n, *_: (0, n))] * outs,
            scratch_shapes=[pltpu.VMEM((rows, len(chunks) * units), jnp.bfloat16)] * 2,
        ),
        out_shape=[jax.ShapeDtypeStruct((rows // outs, width), jnp.float32)] * outs,
        compiler_params=pltpu.CompilerParams(vmem_limit_bytes=grant),
        cost_estimate=light,
        name="reduce",
    )(*([place] if spread else []), *hidden, *pieces, *([] if first else [start]), *([mixed] if spread else []))


def finish_kernel(*refs):
    total = refs[0][...]
    for ref in refs[1:-1]:
        total = total + ref[...]
    refs[-1][...] = total.T


def finish(values):
    channels, width = values[0].shape
    tile = tile_of(width)
    return pl.pallas_call(
        finish_kernel,
        grid=(width // tile,),
        in_specs=[pl.BlockSpec((channels, tile), lambda n: (0, n))] * len(values),
        out_specs=pl.BlockSpec((tile, channels), lambda n: (n, 0)),
        out_shape=jax.ShapeDtypeStruct((width, channels), jnp.float32),
        compiler_params=pltpu.CompilerParams(vmem_limit_bytes=grant),
        cost_estimate=light,
        name="finish",
    )(*values)


def cut_kernel(in_ref, out_ref, own_ref, in_last, out_last):
    rows, units = in_ref.shape[0], own_ref.shape[1]
    own_ref[:rows, :], own_ref[rows:, :] = in_ref[:, :units], out_ref[:, :units]
    in_last[...], out_last[...] = in_ref[:, units:], out_ref[:, units:]


def cut(in_rows, out_rows, units):
    rows, total = in_rows.shape
    whole = pl.BlockSpec((rows, total), lambda n: (0, 0))
    shapes = [(2 * rows, units)] + [(rows, total - units)] * 2
    return pl.pallas_call(
        cut_kernel,
        grid=(1,),
        in_specs=[whole, whole],
        out_specs=[pl.BlockSpec(shape, lambda n: (0, 0)) for shape in shapes],
        out_shape=[jax.ShapeDtypeStruct(shape, jnp.float32) for shape in shapes],
        compiler_params=pltpu.CompilerParams(vmem_limit_bytes=grant),
        cost_estimate=light,
        name="cut",
    )(in_rows, out_rows)


def join(values, axis=0):
    return jnp.concatenate(list(values), axis=axis)


def shards(
    grid,
    fields,
    gain_one,
    tok_in_weight,
    tok_in_bias,
    tok_out_weight,
    gain_two,
    ch_in_weight,
    ch_in_bias,
    ch_out_weight,
):
    ch, deep, move = grid.ch, grid.deep, grid.move
    width = fields.shape[1]
    rows = ch * width // grid.tok
    per_core = width // rows
    core = lax.axis_index("ch")
    z, y, x = grid.place(lax.axis_index("tok"))
    place = jnp.stack([z, y, x, core]).astype(jnp.int32)

    def keys(outer, inner, low=0, high=2):
        fixed = {"y": range(2), "x": range(2), "z": range(deep), outer: range(low, high)}
        names = outer + inner
        return [
            (dict(zip(names, key))["z"], dict(zip(names, key))["y"], dict(zip(names, key))["x"])
            for key in ((o, m, i) for o in fixed[names[0]] for m in fixed[names[1]] for i in fixed[names[2]])
        ]

    def lone(outer, inner):
        return [keys(outer, inner, n, n + 1) for n in range(deep if outer == "z" else 2)]

    whole = keys("z", "yx", 0, deep)
    corner = {(b, a): [key for key in whole if key[1:] == (b, a)] for b in range(2) for a in range(2)}
    y_last = grid.segments([corner[0, 0], corner[0, 1], corner[1, 0], corner[1, 1]], rows)
    x_last = grid.segments([corner[0, 0], corner[1, 0], corner[0, 1], corner[1, 1]], rows)
    y_last_pair = grid.segments([corner[0, 0] + corner[0, 1], corner[1, 0] + corner[1, 1]], rows)
    x_last_pair = grid.segments([corner[0, 0] + corner[1, 0], corner[0, 1] + corner[1, 1]], rows)
    z_after_xy = grid.segments(lone("z", "yx"), rows)
    z_after_yx = grid.segments(lone("z", "xy"), rows)

    units = ch_in_weight.shape[1]
    ends = [units * n // 3 for n in range(4)]
    spans = list(zip(ends, ends[1:]))
    out_rows = ch_out_weight.T

    others = [grid.to_core(fields, ch - step) for step in range(1, ch)]
    pair_gain = jnp.stack([gain_one, gain_two])
    gains = join([pair_gain] + [grid.to_core(pair_gain, ch - step) for step in range(1, ch)], 1).T
    own, in_last, out_last = cut(ch_in_weight, out_rows, ends[2])
    ring = [move(own, dz=1)]
    in_step, out_step = move(in_last, dx=1), move(out_last, dy=1)
    full, high, low = norm_one(grid, place, gains[:, :1], [fields] + others, per_core)
    high, in_step, out_step = fence(high, in_step, out_step)
    in_last, out_last = join([in_last, in_step]), join([out_last, out_step])
    in_step, out_step = move(in_last, dy=1), move(out_last, dx=1)

    middle = tok_in_weight.shape[0] // 2
    quarter = deep * rows
    sent_a, sent_b = mix(high, low, tok_in_weight, False)
    sent_a, sent_b, ring[0], in_step, out_step = fence(sent_a, sent_b, ring[0], in_step, out_step)
    sent_a, sent_b = move(sent_a, dx=1), move(sent_b, dy=1)
    ring.append(move(ring[0], dz=1))
    kept_a, kept_b = mix(high, low, tok_in_weight, True)
    biases = [ch_in_bias[a:b, None] for a, b in spans]
    in_last, out_last = join([in_last, in_step]), join([out_last, out_step])
    sent_a, sent_b, kept_a, kept_b, in_last, out_last, ring[1], *biases = fence(
        sent_a, sent_b, kept_a, kept_b, in_last, out_last, ring[1], *biases
    )
    last_a, last_b = halve([kept_a, sent_a, kept_b, sent_b])
    last_a, last_b = move(last_a, dy=1), move(last_b, dx=1)
    for _ in range(2, deep - 1):
        ring.append(move(ring[-1], dz=1))
    last_a, last_b, ring[-1] = fence(last_a, last_b, ring[-1])

    partial = merge([kept_a, sent_a, last_a, kept_b, sent_b, last_b], deep)
    total = partial[deep - 1]
    for step in range(2, deep + 1):
        total = move(total, dz=1) + partial[deep - step]
    (in_a, in_b), (out_a, out_b) = [[(top, top + rows, a, b) for a, b in spans[:2]] for top in (0, rows)]
    pack_x, pack_y, line_a, line_b = stack(grid.line(own, ring), [in_a, out_b], [in_b, out_a], [in_a], [in_b])
    got_x, got_y = move(pack_x, dx=1), move(pack_y, dy=1)
    in_ring = [move(in_last, dz=1)]
    activated = jax.nn.gelu(total + tok_in_bias[None, :], approximate=False)

    activated, line_a, line_b, got_x, got_y, in_ring[0] = fence(activated, line_a, line_b, got_x, got_y, in_ring[0])
    ring = []
    for step in range(1, deep):
        ring.append(move(ring[-1] if ring else activated, dz=1))
    step_a, step_b = cut_rows([got_x, got_y], quarter)
    first_step = [move(line_a, dy=1), move(step_a, dy=1), move(line_b, dx=1), move(step_b, dx=1)]
    span = tok_out_weight.shape[0]
    out_high, out_low = prepare([tok_out_weight], [[(0, 0, span)]])
    ring[-1], out_high, out_low, *first_step = fence(ring[-1], out_high, out_low, *first_step)
    first = [
        *prepare([line_a, step_a, *first_step[:2]], y_last),
        *prepare([line_b, step_b, *first_step[2:]], x_last),
    ]

    active_a, active_b = stack(grid.line(activated, ring), [(0, rows, 0, middle)], [(0, rows, middle, 2 * middle)])
    lower = quarter, 2 * quarter, 0, ends[1]
    second = [stack([pack_y, got_y], [lower])[0], stack([pack_x, got_x], [lower])[0]]
    arrived = [move(active_a, dy=1), move(active_a, dx=1), move(active_b, dx=1), move(active_b, dy=1)]
    in_ring.append(move(in_ring[0], dz=1))
    in_ring[1], *fenced = fence(in_ring[1], *second, *first, *arrived)
    second, first, arrived = fenced[:2], (fenced[2:4], fenced[4:6]), fenced[6:]
    last_a, last_b = move(arrived[0], dx=1), move(arrived[2], dy=1)
    for _ in range(2, deep - 1):
        in_ring.append(move(in_ring[-1], dz=1))
    most = project(out_high, out_low, [active_a, *arrived[:2], active_b, *arrived[2:]], (0, 2, 1, 0, 1, 2))
    last_a, last_b, in_ring[-1], most = fence(last_a, last_b, in_ring[-1], most)

    second_step = [move(second[0], dx=1), move(second[1], dy=1)]
    out_ring = [move(out_last, dz=1)]
    most = [most] + [grid.to_core(most, step) for step in range(1, ch)]
    least = project(out_high, out_low, [last_a, last_b], (0, 0))
    least = [least] + [grid.to_core(least, step) for step in range(1, ch)]
    terms = [part for pair in zip(most, least) for part in pair]
    mixed, high, low = norm_two(grid, place, gains[:, 1:], full, terms, 2, per_core)

    hidden = [expand(high, low, biases[0], first[0])]
    hidden_high, out_ring[0] = fence(hidden[0][0], out_ring[0])
    hidden[0] = hidden_high, hidden[0][1]
    out_ring.append(move(out_ring[0], dz=1))
    hidden += [
        expand(high, low, biases[1], first[1]),
        expand(high, low, biases[2], grid.line(in_last, in_ring), z_after_xy),
    ]
    fenced = fence(hidden[1][0], hidden[2][0], out_ring[1], *second_step)
    hidden[1:] = [(fenced[0], hidden[1][1]), (fenced[1], hidden[2][1])]
    out_ring[1], *second_step = fenced[2:]
    for _ in range(2, deep - 1):
        out_ring.append(move(out_ring[-1], dz=1))
    (result,) = reduce(
        [
            (hidden[0], [second[0], second_step[0]], x_last_pair),
            (hidden[1], [second[1], second_step[1]], y_last_pair),
        ]
    )
    spread = grid, rows, per_core
    parts = reduce([(hidden[2], grid.line(out_last, out_ring), z_after_yx)], result, spread, place, mixed)
    return finish([parts[0]] + [grid.to_core(part, step) for step, part in enumerate(parts) if step])


def solution(mesh):
    grid = Grid(mesh.shape["tok"], mesh.shape["ch"])
    in_specs = (
        P("tok", "ch"),
        P("ch"),
        P("ch", "tok"),
        P("ch"),
        P("tok", "ch"),
        P("ch"),
        P("tok", "ch"),
        P("ch"),
        P("ch", "tok"),
    )

    def block(*arrays):
        return shards(grid, *arrays)

    return jax.shard_map(block, mesh=mesh, in_specs=in_specs, out_specs=P("tok", "ch"), check_vma=False)
```
